32 devices in a mesh: seq: 8 (over z, y), head: 4 (over x, core).
Axes of the slice: x: 2, y: 2, z: 4, core: 2. Of those that a mesh axis runs over, the one named last changes fastest.
Arguments:
- tokens: bfloat16 [8192, 1024], P('seq'), may hold values from -6 to 6
- cotangent: bfloat16 [8192, 1024], P('seq'), may hold values from -6 to 6
- row_starts: int32 [8192], P('seq'), may hold values from 0 to 1, as said below
- project_weight: float32 [1024, 6144], P('seq', 'head'), may hold values from -0.1875 to 0.1875
- project_first: float32 [1024, 6144], P('seq', 'head'), may hold values from -0.00015258789 to 0.00015258789
- project_second: float32 [1024, 6144], P('seq', 'head'), may hold values from 3.2795209e-09 to 1.3093144e-08
- coeffs_weight: float32 [1024, 24], P('seq', 'head'), may hold values from -0.1875 to 0.1875
- coeffs_first: float32 [1024, 24], P('seq', 'head'), may hold values from -0.00015258789 to 0.00015258789
- coeffs_second: float32 [1024, 24], P('seq', 'head'), may hold values from 3.2795209e-09 to 1.3093144e-08
- kernel_weight: float32 [8, 2560], P('head', 'seq'), may hold values from -3 to 3
- kernel_first: float32 [8, 2560], P('head', 'seq'), may hold values from -0.00015258789 to 0.00015258789
- kernel_second: float32 [8, 2560], P('head', 'seq'), may hold values from 3.2795209e-09 to 1.3093144e-08
- output_weight: float32 [1024, 1024], P('head', 'seq'), may hold values from -0.375 to 0.375
- output_first: float32 [1024, 1024], P('head', 'seq'), may hold values from -0.00015258789 to 0.00015258789
- output_second: float32 [1024, 1024], P('head', 'seq'), may hold values from 3.2795209e-09 to 1.3093144e-08
- expand_weight: float32 [1024, 2, 2816], P('seq', None, 'head'), may hold values from -0.1875 to 0.1875
- expand_first: float32 [1024, 2, 2816], P('seq', None, 'head'), may hold values from -0.00015258789 to 0.00015258789
- expand_second: float32 [1024, 2, 2816], P('seq', None, 'head'), may hold values from 3.2795209e-09 to 1.3093144e-08
- reduce_weight: float32 [2816, 1024], P('head', 'seq'), may hold values from -0.15625 to 0.15625
- reduce_first: float32 [2816, 1024], P('head', 'seq'), may hold values from -0.00015258789 to 0.00015258789
- reduce_second: float32 [2816, 1024], P('head', 'seq'), may hold values from 3.2795209e-09 to 1.3093144e-08
- scales_weight: float32 [2, 1024], P(None, 'seq'), may hold values from 0.4 to 2.2
- scales_first: float32 [2, 1024], P(None, 'seq'), may hold values from -0.00061035156 to 0.00061035156
- scales_second: float32 [2, 1024], P(None, 'seq'), may hold values from 5.2372577e-08 to 2.1198424e-07
- gating_weight: float32 [8, 128], P('head', 'seq'), may hold values from 0.4 to 2.2
- gating_first: float32 [8, 128], P('head', 'seq'), may hold values from -0.00061035156 to 0.00061035156
- gating_second: float32 [8, 128], P('head', 'seq'), may hold values from 5.2372577e-08 to 2.1198424e-07
- decays_weight: float32 [2, 8], replicated, may hold values from -9.5 to 1
- decays_first: float32 [2, 8], replicated, may hold values from -0.00061035156 to 0.00061035156
- decays_second: float32 [2, 8], replicated, may hold values from 5.2372577e-08 to 2.1198424e-07
Outputs:
- layer_output: bfloat16 [8192, 1024], P('seq')
- input_grad: bfloat16 [8192, 1024], P('seq')
- project_master: float32 [1024, 6144], P('seq', 'head')
- project_moment: float32 [1024, 6144], P('seq', 'head')
- project_square: float32 [1024, 6144], P('seq', 'head')
- project_copy: bfloat16 [1024, 6144], P('seq', 'head')
- coeffs_master: float32 [1024, 24], P('seq', 'head')
- coeffs_moment: float32 [1024, 24], P('seq', 'head')
- coeffs_square: float32 [1024, 24], P('seq', 'head')
- coeffs_copy: bfloat16 [1024, 24], P('seq', 'head')
- kernel_master: float32 [8, 2560], P('head', 'seq')
- kernel_moment: float32 [8, 2560], P('head', 'seq')
- kernel_square: float32 [8, 2560], P('head', 'seq')
- kernel_copy: bfloat16 [8, 2560], P('head', 'seq')
- output_master: float32 [1024, 1024], P('head', 'seq')
- output_moment: float32 [1024, 1024], P('head', 'seq')
- output_square: float32 [1024, 1024], P('head', 'seq')
- output_copy: bfloat16 [1024, 1024], P('head', 'seq')
- expand_master: float32 [1024, 2, 2816], P('seq', None, 'head')
- expand_moment: float32 [1024, 2, 2816], P('seq', None, 'head')
- expand_square: float32 [1024, 2, 2816], P('seq', None, 'head')
- expand_copy: bfloat16 [1024, 2, 2816], P('seq', None, 'head')
- reduce_master: float32 [2816, 1024], P('head', 'seq')
- reduce_moment: float32 [2816, 1024], P('head', 'seq')
- reduce_square: float32 [2816, 1024], P('head', 'seq')
- reduce_copy: bfloat16 [2816, 1024], P('head', 'seq')
- scales_master: float32 [2, 1024], P(None, 'seq')
- scales_moment: float32 [2, 1024], P(None, 'seq')
- scales_square: float32 [2, 1024], P(None, 'seq')
- gating_master: float32 [8, 128], P('head', 'seq')
- gating_moment: float32 [8, 128], P('head', 'seq')
- gating_square: float32 [8, 128], P('head', 'seq')
- decays_master: float32 [2, 8], replicated
- decays_moment: float32 [2, 8], replicated
- decays_square: float32 [2, 8], replicated
- grad_norm: float32 [], replicated
The draws below stay inside these ranges and needn't reach their ends.
Inputs may be any that keep to these rules, and one draw needn't show every extreme that they name: `row_starts`: 1 at the first token of each row and 0 elsewhere; token 0 starts a row; every row holds 1024 tokens or more.
All inputs are finite; a program needn't handle non-finite values.
Results may differ from the reference program's by a relative error of at most 0.02.
Values may be sent and summed in bfloat16 or wider, within the bound.
A program may use at most 192 MiB of HBM per device.

```python
import math
import jax
import jax.numpy as jnp
from jax import lax

D = 1024
H = 8
DK = 128
FF = 2816
NH = 2
CONV = 4
STRETCH = 64
STEP = 10
MIN_ROW = 1024
TOKENS = 8192
NPARAM = 16038928


def draw_row_starts(key, part):
    key = jax.random.fold_in(key, 1)
    row_count = max(2, TOKENS // (4 * MIN_ROW))
    spare = TOKENS - row_count * MIN_ROW
    cuts = jnp.sort(jax.random.randint(key, (row_count - 1,), 0, spare + 1))
    bounds = jnp.concatenate([jnp.zeros((1,), jnp.int32), cuts.astype(jnp.int32), jnp.full((1,), spare, jnp.int32)])
    lengths = MIN_ROW + (bounds[1:] - bounds[:-1])
    begins = jnp.concatenate([jnp.zeros((1,), jnp.int32), jnp.cumsum(lengths)[:-1].astype(jnp.int32)])
    return jnp.zeros((TOKENS,), jnp.int32).at[begins].set(1)


def rising_gains(key, rows, columns, along_rows):
    if along_rows:
        ramp = 0.6 + 1.2 * jnp.arange(rows, dtype=jnp.float32)[:, None] / rows
    else:
        ramp = 0.6 + 1.2 * jnp.arange(columns, dtype=jnp.float32)[None, :] / columns
    noise = 1.0 + 0.1 * jnp.clip(jax.random.normal(key, (rows, columns), jnp.float32), -2.0, 2.0)
    return ramp * noise


def draw_scales_weight(key, part):
    key = jax.random.fold_in(key, 2)
    return rising_gains(key, 2, D, False)


def draw_gating_weight(key, part):
    key = jax.random.fold_in(key, 3)
    return rising_gains(key, H, DK, True)


def draw_decays_weight(key, part):
    key = jax.random.fold_in(key, 4)
    rate_key, bias_key = jax.random.split(key)
    rates = jax.random.uniform(rate_key, (H,), jnp.float32, -9.5, -3.0)
    biases = jax.random.uniform(bias_key, (H,), jnp.float32, -1.0, 1.0)
    return jnp.stack([rates, biases])


def strengthened(values, stream_key, source, target, blocks, factor):
    def block_of(axis_at):
        return (jnp.arange(values.shape[axis_at]) // (values.shape[axis_at] // blocks)).reshape((-1,) + (1,) * (values.ndim - 1 - axis_at))

    near = jax.random.permutation(stream_key, blocks)[block_of(target)]
    second = (block_of(target) + blocks // 2) % blocks
    return jnp.where((block_of(source) == near) | (block_of(source) == second), factor * values, values)


def steps_of(key, dims, shards, smallest, largest):
    level = 1.0
    for dim, parts in shards:
        steps = jax.random.uniform(jax.random.fold_in(jax.random.fold_in(key, 6), dim), (parts,), jnp.float32, smallest / len(shards), largest / len(shards))
        level = level * jnp.repeat(jnp.exp(steps), dims[dim] // parts).reshape((-1,) + (1,) * (len(dims) - 1 - dim))
    return level


def centred(stream_key, shape, scale, reach, cuts=(), held_as=jnp.bfloat16):
    array = scale * jax.random.normal(stream_key, shape, jnp.float32)
    if cuts:
        array = array * steps_of(stream_key, shape, cuts, -0.22, 0.18)
    return jnp.clip(array, -reach, reach).astype(held_as)


def gaussian_with(rng, dims, deviation, reach, cuts, heavy, kind=jnp.bfloat16):
    entries = deviation * jax.random.normal(rng, dims, jnp.float32)
    if cuts:
        entries = entries * steps_of(rng, dims, cuts, -0.22, 0.18)
    return jnp.clip(strengthened(entries, jax.random.fold_in(rng, 3), *heavy), -reach, reach).astype(kind)


def setup_inputs(seed: int = 0) -> dict:
    key_list = jax.random.split(jax.random.key(seed), 31)
    tokens = gaussian_with(key_list[0], (TOKENS, D), 1.0, 6.0, ((0, 8),), (0, 1, 8, 2.0))
    cotangent = gaussian_with(key_list[1], (TOKENS, D), 1.0, 6.0, ((0, 8),), (0, 1, 8, 2.0))
    row_starts = draw_row_starts(jax.random.fold_in(key_list[30], 71), 0)
    project_weight = centred(key_list[3], (D, H * (2 + 2 * NH) * DK), D ** -0.5, 0.1875, ((0, 8), (1, 4)), jnp.float32)
    project_first = centred(key_list[4], (D, H * (2 + 2 * NH) * DK), (0.111 * NPARAM ** -0.5), 0.00015258789, ((0, 8), (1, 4)), jnp.float32)
    project_second = jnp.clip(jnp.exp(math.log(1.3093144346498775e-08) - 1.3843914 * jax.random.uniform(key_list[5], (D, H * (2 + 2 * NH) * DK), jnp.float32) ** steps_of(key_list[5], (D, H * (2 + 2 * NH) * DK), ((0, 8), (1, 4)), -0.2, 0.2)), 3.2795208770863837e-09, 1.3093144346498775e-08)
    coeffs_weight = centred(key_list[6], (D, H * (NH + 1)), D ** -0.5, 0.1875, ((0, 8), (1, 4)), jnp.float32)
    coeffs_first = centred(key_list[7], (D, H * (NH + 1)), (0.111 * NPARAM ** -0.5), 0.00015258789, ((0, 8), (1, 4)), jnp.float32)
    coeffs_second = jnp.clip(jnp.exp(math.log(1.3093144346498775e-08) - 1.3843914 * jax.random.uniform(key_list[8], (D, H * (NH + 1)), jnp.float32) ** steps_of(key_list[8], (D, H * (NH + 1)), ((0, 8), (1, 4)), -0.2, 0.2)), 3.2795208770863837e-09, 1.3093144346498775e-08)
    kernel_weight = centred(key_list[9], (H, (1 + 2 * NH) * DK * CONV), CONV ** -0.5, 3.0, ((0, 4), (1, 8)), jnp.float32)
    kernel_first = centred(key_list[10], (H, (1 + 2 * NH) * DK * CONV), (0.111 * NPARAM ** -0.5), 0.00015258789, ((0, 4), (1, 8)), jnp.float32)
    kernel_second = jnp.clip(jnp.exp(math.log(1.3093144346498775e-08) - 1.3843914 * jax.random.uniform(key_list[11], (H, (1 + 2 * NH) * DK * CONV), jnp.float32) ** steps_of(key_list[11], (H, (1 + 2 * NH) * DK * CONV), ((0, 4), (1, 8)), -0.2, 0.2)), 3.2795208770863837e-09, 1.3093144346498775e-08)
    output_weight = centred(key_list[12], (H * DK, D), (H * DK // 4) ** -0.5, 0.375, ((0, 4), (1, 8)), jnp.float32)
    output_first = centred(key_list[13], (H * DK, D), (0.111 * NPARAM ** -0.5), 0.00015258789, ((0, 4), (1, 8)), jnp.float32)
    output_second = jnp.clip(jnp.exp(math.log(1.3093144346498775e-08) - 1.3843914 * jax.random.uniform(key_list[14], (H * DK, D), jnp.float32) ** steps_of(key_list[14], (H * DK, D), ((0, 4), (1, 8)), -0.2, 0.2)), 3.2795208770863837e-09, 1.3093144346498775e-08)
    expand_weight = centred(key_list[15], (D, 2, FF), D ** -0.5, 0.1875, ((0, 8), (2, 4)), jnp.float32)
    expand_first = centred(key_list[16], (D, 2, FF), (0.111 * NPARAM ** -0.5), 0.00015258789, ((0, 8), (2, 4)), jnp.float32)
    expand_second = jnp.clip(jnp.exp(math.log(1.3093144346498775e-08) - 1.3843914 * jax.random.uniform(key_list[17], (D, 2, FF), jnp.float32) ** steps_of(key_list[17], (D, 2, FF), ((0, 8), (2, 4)), -0.2, 0.2)), 3.2795208770863837e-09, 1.3093144346498775e-08)
    reduce_weight = centred(key_list[18], (FF, D), (FF // 2) ** -0.5, 0.15625, ((0, 4), (1, 8)), jnp.float32)
    reduce_first = centred(key_list[19], (FF, D), (0.111 * NPARAM ** -0.5), 0.00015258789, ((0, 4), (1, 8)), jnp.float32)
    reduce_second = jnp.clip(jnp.exp(math.log(1.3093144346498775e-08) - 1.3843914 * jax.random.uniform(key_list[20], (FF, D), jnp.float32) ** steps_of(key_list[20], (FF, D), ((0, 4), (1, 8)), -0.2, 0.2)), 3.2795208770863837e-09, 1.3093144346498775e-08)
    scales_weight = draw_scales_weight(jax.random.fold_in(key_list[30], 71), 0)
    scales_first = centred(key_list[22], (2, D), (0.444 * NPARAM ** -0.5), 0.00061035156, ((1, 8),), jnp.float32)
    scales_second = jnp.clip(jnp.exp(math.log(2.1198424349222478e-07) - 1.39812883 * jax.random.uniform(key_list[23], (2, D), jnp.float32) ** steps_of(key_list[23], (2, D), ((1, 8),), -0.2, 0.2)), 5.23725773859951e-08, 2.1198424349222478e-07)
    gating_weight = draw_gating_weight(jax.random.fold_in(key_list[30], 71), 0)
    gating_first = centred(key_list[25], (H, DK), (0.444 * NPARAM ** -0.5), 0.00061035156, ((0, 4), (1, 8)), jnp.float32)
    gating_second = jnp.clip(jnp.exp(math.log(2.1198424349222478e-07) - 1.39812883 * jax.random.uniform(key_list[26], (H, DK), jnp.float32) ** steps_of(key_list[26], (H, DK), ((0, 4), (1, 8)), -0.2, 0.2)), 5.23725773859951e-08, 2.1198424349222478e-07)
    decays_weight = draw_decays_weight(jax.random.fold_in(key_list[30], 71), 0)
    decays_first = centred(key_list[28], (2, H), (0.444 * NPARAM ** -0.5), 0.00061035156, (), jnp.float32)
    decays_second = jnp.clip(jnp.exp(jax.random.uniform(key_list[29], (2, H), jnp.float32, math.log(5.23725773859951e-08), math.log(2.1198424349222478e-07))), 5.23725773859951e-08, 2.1198424349222478e-07)
    return {"tokens": tokens, "cotangent": cotangent, "row_starts": row_starts, "project_weight": project_weight, "project_first": project_first, "project_second": project_second, "coeffs_weight": coeffs_weight, "coeffs_first": coeffs_first, "coeffs_second": coeffs_second, "kernel_weight": kernel_weight, "kernel_first": kernel_first, "kernel_second": kernel_second, "output_weight": output_weight, "output_first": output_first, "output_second": output_second, "expand_weight": expand_weight, "expand_first": expand_first, "expand_second": expand_second, "reduce_weight": reduce_weight, "reduce_first": reduce_first, "reduce_second": reduce_second, "scales_weight": scales_weight, "scales_first": scales_first, "scales_second": scales_second, "gating_weight": gating_weight, "gating_first": gating_first, "gating_second": gating_second, "decays_weight": decays_weight, "decays_first": decays_first, "decays_second": decays_second}


EPS_NORM = 1e-06
EPS_KEY = 1e-06
BETA_ONE = 0.9
BETA_TWO = 0.95
ADAM_EPS = 1e-08
LEARN_RATE = 0.02
KERNEL_RATE = 0.3
GAIN_RATE = 0.8
DECAY_RATE = 2.5
WEIGHT_DECAY = 0.1
CLIP_NORM = 1.0
STEP_OFFSET = -2.5
HIGH = lax.Precision.HIGHEST

@jax.custom_vjp
def low(v):
    return lax.optimization_barrier(v.astype(jnp.bfloat16)).astype(jnp.float32)

@jax.custom_vjp
def low_back(v):
    return v

def low_keep(v):
    return (low(v), None)

def low_pass(kept, grad):
    return (grad,)

def back_keep(v):
    return (v, None)

def back_low(kept, grad):
    return (low(grad),)
low.defvjp(low_keep, low_pass)
low_back.defvjp(back_keep, back_low)

def product(spec, left, right):
    return jnp.einsum(spec, left, right, precision=HIGH)

def normalize(values, gains):
    return values * lax.rsqrt(lax.optimization_barrier(jnp.mean(values * values, -1, keepdims=True)) + EPS_NORM) * gains

def conv_mix(conv_in, history, kernel, starts):
    length = conv_in.shape[0]
    padded = jnp.concatenate([history, conv_in], 0)
    counts = jnp.cumsum(starts).astype(jnp.int32)
    summed = conv_in * kernel[:, :, CONV - 1]
    for offset in range(1, CONV):
        shifted = padded[CONV - 1 - offset:CONV - 1 - offset + length]
        earlier = jnp.concatenate([jnp.zeros((offset,), jnp.int32), counts[:length - offset]], 0)
        summed = summed + jnp.where((counts - earlier == 0)[:, None, None], shifted, 0.0) * kernel[:, :, CONV - 1 - offset]
    return jax.nn.silu(summed)

def head_inputs(activated, coeffs_in, decay_in):
    length, head_count = (activated.shape[0], activated.shape[1])
    queries = activated[:, :, :DK]
    key_parts = activated[:, :, DK:(1 + NH) * DK].reshape(length, head_count, NH, DK)
    value_parts = activated[:, :, (1 + NH) * DK:].reshape(length, head_count, NH, DK)
    key_parts = key_parts * lax.rsqrt(lax.optimization_barrier(jnp.sum(key_parts * key_parts, -1, keepdims=True)) + EPS_KEY)
    coeffs_in = coeffs_in.reshape(length, head_count, NH + 1)
    strength = jax.nn.sigmoid(coeffs_in[:, :, :NH] + STEP_OFFSET)
    log_rate = -jnp.exp(decay_in[0])[None, :] * jax.nn.softplus(coeffs_in[:, :, NH] + decay_in[1][None, :])
    log_steps = jnp.concatenate([log_rate[:, :, None], jnp.zeros((length, head_count, NH - 1), jnp.float32)], -1)
    return (queries, key_parts, value_parts, strength, log_steps)

def to_blocks(queries, key_parts, value_parts, strength, log_steps, starts):
    length, head_count = (queries.shape[0], queries.shape[1])
    block_count = length // STRETCH
    step_count = STRETCH * NH
    query_blocks = queries.transpose(1, 0, 2).reshape(head_count, block_count, STRETCH, DK)
    key_blocks = key_parts.transpose(1, 0, 2, 3).reshape(head_count, block_count, step_count, DK)
    value_blocks = value_parts.transpose(1, 0, 2, 3).reshape(head_count, block_count, step_count, DK)
    beta_blocks = strength.transpose(1, 0, 2).reshape(head_count, block_count, step_count)
    log_blocks = log_steps.transpose(1, 0, 2).reshape(head_count, block_count, step_count)
    resets = jnp.concatenate([starts[:, None], jnp.zeros((length, NH - 1), jnp.int32)], 1).reshape(block_count, step_count)
    return (query_blocks, key_blocks, value_blocks, beta_blocks, log_blocks, resets)

def block_parts(key_blocks, value_blocks, beta_blocks, log_blocks, resets):
    step_count = key_blocks.shape[-2]
    cumulated = jnp.cumsum(log_blocks, axis=-1)
    segment = jnp.cumsum(resets, axis=-1).astype(jnp.int32)
    row_ids = lax.broadcasted_iota(jnp.int32, (step_count, step_count), 0)
    col_ids = lax.broadcasted_iota(jnp.int32, (step_count, step_count), 1)
    same_row = (segment[..., :, None] == segment[..., None, :]) & (row_ids >= col_ids)
    strict = same_row & (row_ids > col_ids)
    log_gap = jnp.where(same_row, cumulated[..., :, None] - cumulated[..., None, :], 0.0)
    retain = jnp.where(same_row, jnp.exp(log_gap), 0.0)
    initial = jnp.where(segment == 0, jnp.exp(cumulated), 0.0)
    key_gram = product('...ik,...jk->...ij', key_blocks, key_blocks)
    triangle = jnp.where(strict, beta_blocks[..., :, None] * retain * key_gram, 0.0) + jnp.eye(step_count, dtype=jnp.float32)
    update = jax.scipy.linalg.solve_triangular(triangle, beta_blocks[..., None] * value_blocks, lower=True, unit_diagonal=True)
    carried = jax.scipy.linalg.solve_triangular(triangle, (beta_blocks * initial)[..., None] * key_blocks, lower=True, unit_diagonal=True)
    last_row = retain[..., step_count - 1, :]
    transfer = initial[..., step_count - 1][..., None, None] * jnp.eye(DK, dtype=jnp.float32) - product('...jk,...jl->...kl', key_blocks, last_row[..., None] * carried)
    offset = product('...jk,...jl->...kl', key_blocks, last_row[..., None] * update)
    return (retain, initial, update, carried, transfer, offset)

def block_out(query_blocks, key_blocks, retain, initial, update, carried, current):
    picked = retain[..., NH - 1::NH, :]
    leading = initial[..., NH - 1::NH]
    deltas = update - product('...ik,...kl->...il', carried, current)
    scores = product('...ik,...jk->...ij', query_blocks, key_blocks) * picked
    return leading[..., None] * product('...ik,...kl->...il', query_blocks, current) + product('...ij,...jl->...il', scores, deltas)

def finish(results, gate_in, gating):
    scaled = results * lax.rsqrt(lax.optimization_barrier(jnp.mean(results * results, -1, keepdims=True)) + EPS_NORM)
    return scaled * gating[None] * jax.nn.silu(gate_in)

def mixer_branch(normed, project, coeffs, kernel, output, gating, decays, starts):
    length = normed.shape[0]
    width = (1 + 2 * NH) * DK
    projected = low_back(low(jnp.dot(normed, project, precision=HIGH))).reshape(length, H, (2 + 2 * NH) * DK)
    coeffs_out = low_back(low(jnp.dot(normed, coeffs, precision=HIGH)))
    history = jnp.zeros((CONV - 1, H, width), jnp.float32)
    activated = conv_mix(projected[:, :, :width], history, kernel.reshape(H, width, CONV), starts)
    queries, key_parts, value_parts, strength, log_steps = head_inputs(activated, coeffs_out, decays)
    query_blocks, key_blocks, value_blocks, beta_blocks, log_blocks, resets = to_blocks(queries, key_parts, value_parts, strength, log_steps, starts)

    def stretch_step(current, element):
        query_one, key_one, value_one, beta_one, log_one, reset_one = element
        retain, initial, update, carried, transfer, offset = block_parts(key_one, value_one, beta_one, log_one, reset_one)
        result = block_out(query_one, key_one, retain, initial, update, carried, current)
        return (product('...kl,...lm->...km', transfer, current) + offset, result)
    initial_state = jnp.zeros((H, DK, DK), jnp.float32)
    unused, results = lax.scan(jax.checkpoint(stretch_step), initial_state, (jnp.moveaxis(query_blocks, 1, 0), jnp.moveaxis(key_blocks, 1, 0), jnp.moveaxis(value_blocks, 1, 0), jnp.moveaxis(beta_blocks, 1, 0), jnp.moveaxis(log_blocks, 1, 0), resets))
    results = jnp.moveaxis(results, 0, 1).reshape(H, length, DK).transpose(1, 0, 2)
    gated = low(finish(results, projected[:, :, width:], gating)).reshape(length, H * DK)
    return low_back(jnp.dot(gated, output, precision=HIGH))

def residual_block(inputs, project, coeffs, kernel, output, expand, shrink, scales, gating, decays, starts):
    project = low(project)
    coeffs = low(coeffs)
    kernel = low(kernel)
    output = low(output)
    expand = low(expand)
    shrink = low(shrink)
    scales = low(scales)
    gating = low(gating)
    decays = low(decays)
    normed = low(normalize(inputs, scales[0]))
    middle = inputs + mixer_branch(normed, project, coeffs, kernel, output, gating, decays, starts)
    second = low(normalize(middle, scales[1]))
    gate_up = low_back(product('nd,dgf->ngf', second, expand))
    hidden = low(jax.nn.silu(gate_up[:, 0]) * gate_up[:, 1])
    return middle + low_back(jnp.dot(hidden, shrink, precision=HIGH))

def adamw(weight, first, second, gradient, factor, step_rate, decay_rate):
    gradient = gradient * factor
    moment = BETA_ONE * first + (1.0 - BETA_ONE) * gradient
    square = BETA_TWO * second + (1.0 - BETA_TWO) * gradient * gradient
    scaled = moment / (1.0 - BETA_ONE ** STEP)
    spread = jnp.sqrt(square / (1.0 - BETA_TWO ** STEP))
    master = weight - step_rate * (scaled / (spread + ADAM_EPS) + decay_rate * weight)
    return (master, moment, square)

def reference(tokens, cotangent, row_starts, project_weight, project_first, project_second, coeffs_weight, coeffs_first, coeffs_second, kernel_weight, kernel_first, kernel_second, output_weight, output_first, output_second, expand_weight, expand_first, expand_second, reduce_weight, reduce_first, reduce_second, scales_weight, scales_first, scales_second, gating_weight, gating_first, gating_second, decays_weight, decays_first, decays_second):

    def forward(inputs, project, coeffs, kernel, output, expand, shrink, scales, gating, decays):
        return residual_block(inputs, project, coeffs, kernel, output, expand, shrink, scales, gating, decays, row_starts)
    result, pullback = jax.vjp(forward, tokens.astype(jnp.float32), project_weight, coeffs_weight, kernel_weight, output_weight, expand_weight, reduce_weight, scales_weight, gating_weight, decays_weight)
    gradients = pullback(cotangent.astype(jnp.float32))
    squares = jnp.stack([jnp.sum(gradient * gradient) for gradient in gradients[1:]])
    grad_norm = jnp.sqrt(jnp.sum(squares))
    factor = jnp.minimum(1.0, CLIP_NORM / (grad_norm + 1e-06))
    project_new = adamw(project_weight, project_first, project_second, gradients[1], factor, LEARN_RATE, WEIGHT_DECAY)
    coeffs_new = adamw(coeffs_weight, coeffs_first, coeffs_second, gradients[2], factor, LEARN_RATE, WEIGHT_DECAY)
    kernel_new = adamw(kernel_weight, kernel_first, kernel_second, gradients[3], factor, KERNEL_RATE, WEIGHT_DECAY)
    output_new = adamw(output_weight, output_first, output_second, gradients[4], factor, LEARN_RATE, WEIGHT_DECAY)
    expand_new = adamw(expand_weight, expand_first, expand_second, gradients[5], factor, LEARN_RATE, WEIGHT_DECAY)
    reduce_new = adamw(reduce_weight, reduce_first, reduce_second, gradients[6], factor, LEARN_RATE, WEIGHT_DECAY)
    scales_new = adamw(scales_weight, scales_first, scales_second, gradients[7], factor, GAIN_RATE, 0.0)
    gating_new = adamw(gating_weight, gating_first, gating_second, gradients[8], factor, GAIN_RATE, 0.0)
    decays_new = adamw(decays_weight, decays_first, decays_second, gradients[9], factor, DECAY_RATE, 0.0)
    return (result.astype(jnp.bfloat16), gradients[0].astype(jnp.bfloat16), project_new[0], project_new[1], project_new[2], project_new[0].astype(jnp.bfloat16), coeffs_new[0], coeffs_new[1], coeffs_new[2], coeffs_new[0].astype(jnp.bfloat16), kernel_new[0], kernel_new[1], kernel_new[2], kernel_new[0].astype(jnp.bfloat16), output_new[0], output_new[1], output_new[2], output_new[0].astype(jnp.bfloat16), expand_new[0], expand_new[1], expand_new[2], expand_new[0].astype(jnp.bfloat16), reduce_new[0], reduce_new[1], reduce_new[2], reduce_new[0].astype(jnp.bfloat16), scales_new[0], scales_new[1], scales_new[2], gating_new[0], gating_new[1], gating_new[2], decays_new[0], decays_new[1], decays_new[2], grad_norm)
```

```python
import jax
import jax.numpy as jnp
import numpy as np
from jax import lax
from jax.experimental import pallas as pl
from jax.experimental.pallas import tpu as pltpu
from jax.sharding import PartitionSpec as P

H = 8
DK = 128
NH = 2
CONV = 4
STRETCH = 64
STEP = 10


EPS_NORM = 1e-06
EPS_KEY = 1e-06
BETA_ONE = 0.9
BETA_TWO = 0.95
ADAM_EPS = 1e-08
LEARN_RATE = 0.02
KERNEL_RATE = 0.3
GAIN_RATE = 0.8
DECAY_RATE = 2.5
WEIGHT_DECAY = 0.1
CLIP_NORM = 1.0
STEP_OFFSET = -2.5


MESH = pl.DeviceIdType.MESH


def place_of(index, count):
    return jnp.where(index % 2 == 0, index // 2, count - 1 - index // 2)


def index_of(place, count):
    place = (place + 2 * count) % count
    return jnp.where(place < count // 2, 2 * place, 2 * (count - 1 - place) + 1)


def greet(partners):
    barrier = pltpu.get_barrier_semaphore()
    for partner in partners:
        pl.semaphore_signal(barrier, inc=1, device_id=partner, device_id_type=MESH)
    pl.semaphore_wait(barrier, len(partners))


def remote(source, target, send, receive, device):
    return pltpu.make_async_remote_copy(
        src_ref=source,
        dst_ref=target,
        send_sem=send,
        recv_sem=receive,
        device_id=device,
        device_id_type=MESH,
    )


def ring_neighbours(count):
    place = place_of(lax.axis_index("seq"), count)
    return (
        {"seq": index_of(place + 1, count)},
        {"seq": index_of(place - 1, count)},
    )


def head_neighbours():
    me = lax.axis_index("head")
    members = lax.axis_size("head")
    return {"head": me + 1 - 2 * (me % 2)}, {"head": (me + members // 2) % members}


class Gather:
    def __init__(self, count, items, send, receive):
        self.count, self.items, self.send, self.receive = count, items, send, receive
        self.steps = count // 2
        self.place = place_of(lax.axis_index("seq"), count)
        self.devices = ring_neighbours(count)

    def origin(self, step, way):
        return index_of(self.place - step if way == 0 else self.place + step, self.count)

    def keys(self, step, group):
        return [
            (number, way)
            for number in (range(len(self.items)) if group is None else group)
            for way in range(2)
            if step < self.steps - 1 or number % 2 == way
        ]

    def copy(self, step, number, way):
        own, whole, cut = self.items[number]
        target = whole.at[(self.origin(step, way), *cut)]
        return remote(
            own.at[cut] if step == 0 else target,
            target,
            self.send.at[number, way, step],
            self.receive.at[number, way, step],
            self.devices[way],
        )

    def advance(self, step, group=None):
        going = self.keys(step, group)
        for key in going:
            if step:
                self.copy(step - 1, *key).wait_recv()
            self.copy(step, *key).start()
        if step:
            for key in self.keys(step - 1, group):
                if key not in going:
                    self.copy(step - 1, *key).wait_recv()

    def arrive(self, step):
        for key in self.keys(step, None):
            self.copy(step, *key).wait_recv()

    def drain(self):
        for step in range(self.steps):
            for key in self.keys(step, None):
                self.copy(step, *key).wait_send()


def pieces(own, whole, parts):
    size = own.shape[-1]
    lead = (slice(None),) * (len(own.shape) - 1)
    marks = [size // 128 * i // parts * 128 for i in range(parts)] + [size]
    return [
        (own, whole, lead + (slice(a, b),)) for a, b in zip(marks[:-1], marks[1:]) if a < b
    ]


class Scatter:
    def __init__(self, count, parts, slots, staged, cuts, send, receive):
        self.count, self.parts, self.slots, self.staged = count, parts, slots, staged
        self.cuts, self.send, self.receive = cuts, send, receive
        self.steps = count - 1
        self.place = place_of(lax.axis_index("seq"), count)
        self.devices = ring_neighbours(count)

    def owner(self, step, way):
        return index_of(
            self.place - 1 - step if way == 0 else self.place + 1 + step, self.count
        )

    def copy(self, step, number):
        which, start, size, way = self.cuts[number]
        columns = slice(start, start + size)
        if step == 0:
            source = self.parts[which].at[self.owner(step, way), :, columns]
        else:
            source = self.staged[which].at[step - 1, :, columns]
        return remote(
            source,
            self.slots[which].at[step, :, columns],
            self.send.at[number, step],
            self.receive.at[number, step],
            self.devices[way],
        )

    def start(self, step, group=None):
        for number, (which, start, size, way) in enumerate(self.cuts):
            if group is not None and number not in group:
                continue
            columns = slice(start, start + size)
            if step:
                self.copy(step - 1, number).wait_recv()
                self.staged[which][step - 1, :, columns] = (
                    self.slots[which][step - 1, :, columns]
                    + self.parts[which][self.owner(step, way), :, columns]
                )
            self.copy(step, number).start()

    def finish(self, totals):
        me = lax.axis_index("seq")
        for number, (which, start, size, way) in enumerate(self.cuts):
            columns = slice(start, start + size)
            self.copy(self.steps - 1, number).wait_recv()
            totals[which][:, columns] = self.slots[which][self.steps - 1, :, columns].astype(
                jnp.float32
            ) + self.parts[which][me, :, columns].astype(jnp.float32)
        for step in range(self.steps):
            for number in range(len(self.cuts)):
                self.copy(step, number).wait_send()


def scatter_cuts(widths, pieces_of):
    cuts = []
    for which, (columns, parts) in enumerate(zip(widths, pieces_of)):
        marks = [columns // 128 * i // parts * 128 for i in range(parts)] + [columns]
        for number in range(parts):
            if marks[number] < marks[number + 1]:
                cuts.append((which, marks[number], marks[number + 1] - marks[number], number % 2))
    return cuts


def scatter_scratch(count, rows, widths, pieces_of):
    passing = [
        pltpu.VMEM((count - 1, each, columns), jnp.bfloat16) for each, columns in zip(rows, widths)
    ]
    cuts = len(scatter_cuts(widths, pieces_of))
    return [
        *passing,
        *passing,
        pltpu.SemaphoreType.DMA((cuts, count - 1)),
        pltpu.SemaphoreType.DMA((cuts, count - 1)),
    ]


CUT = 8


class HeadSum:
    def __init__(self, part, total, near, half, far, send, receive):
        self.part, self.total, self.near, self.half, self.far = part, total, near, half, far
        self.send, self.receive = send, receive
        me = lax.axis_index("head")
        self.twin, self.across = head_neighbours()
        self.rows = part.shape[0] // 2
        self.size = self.rows // CUT
        self.mine = (me % 2) * self.rows
        self.other = self.rows - self.mine

    def copy(self, stage, cut):
        span = pl.ds(pl.multiple_of(cut * self.size, self.size), self.size)
        here = pl.ds(pl.multiple_of(self.mine + cut * self.size, self.size), self.size)
        there = pl.ds(pl.multiple_of(self.other + cut * self.size, self.size), self.size)
        pairs = (
            (self.part.at[there], self.near.at[span], self.twin),
            (self.half.at[span], self.far.at[span], self.across),
            (self.total.at[here], self.total.at[here], self.twin),
        )
        source, target, device = pairs[stage]
        return remote(
            source, target, self.send.at[stage, cut], self.receive.at[stage, cut], device
        )

    def first(self, cuts=range(CUT)):
        for cut in cuts:
            self.copy(0, cut).start()

    def second(self, cuts=range(CUT)):
        for cut in cuts:
            span = pl.ds(pl.multiple_of(cut * self.size, self.size), self.size)
            here = pl.ds(pl.multiple_of(self.mine + cut * self.size, self.size), self.size)
            self.copy(0, cut).wait_recv()
            self.half[span] = self.part[here] + self.near[span]
            self.copy(1, cut).start()

    def third(self, cuts=range(CUT)):
        for cut in cuts:
            span = pl.ds(pl.multiple_of(cut * self.size, self.size), self.size)
            here = pl.ds(pl.multiple_of(self.mine + cut * self.size, self.size), self.size)
            self.copy(1, cut).wait_recv()
            self.total[here] = self.half[span] + self.far[span]
            self.copy(2, cut).start()

    def landed(self, cuts=range(CUT)):
        for cut in cuts:
            self.copy(2, cut).wait_recv()

    def flush(self):
        for stage in range(3):
            for cut in range(CUT):
                self.copy(stage, cut).wait_send()

    def finish(self):
        self.landed()
        self.flush()


class ChunkSum:
    def __init__(self, count, part, total, near, half, far, send, receive):
        self.count, self.part, self.total = count, part, total
        self.near, self.half, self.far = near, half, far
        self.send, self.receive = send, receive
        self.side = lax.axis_index("head") % 2
        self.twin, self.across = head_neighbours()

    def sums(self, chunk):
        return self.side == (1 if chunk < self.count // 2 else 0)

    def copy(self, stage, chunk):
        source, target, device = (
            (self.part, self.near, self.twin),
            (self.half, self.far, self.across),
            (self.total, self.total, self.twin),
        )[stage]
        return remote(
            source.at[chunk],
            target.at[chunk],
            self.send.at[stage, chunk],
            self.receive.at[stage, chunk],
            device,
        )

    def first(self, chunk):
        @pl.when(jnp.logical_not(self.sums(chunk)))
        def _():
            self.copy(0, chunk).start()

    def second(self, chunk):
        @pl.when(self.sums(chunk))
        def _():
            self.copy(0, chunk).wait_recv()
            self.half[chunk] = self.part[chunk] + self.near[chunk]
            self.copy(1, chunk).start()

    def third(self, chunk):
        @pl.when(self.sums(chunk))
        def _():
            self.copy(1, chunk).wait_recv()
            self.total[chunk] = self.half[chunk] + self.far[chunk]
            self.copy(2, chunk).start()

    def finish(self):
        for chunk in range(self.count):

            @pl.when(self.sums(chunk))
            def _():
                self.copy(1, chunk).wait_send()
                self.copy(2, chunk).wait_send()

            @pl.when(jnp.logical_not(self.sums(chunk)))
            def _():
                self.copy(0, chunk).wait_send()
                self.copy(2, chunk).wait_recv()


class Spread:
    def __init__(self, blocks, own, cuts, send, receive):
        self.blocks, self.own, self.cuts = blocks, own, cuts
        self.send, self.receive = send, receive
        self.me = lax.axis_index("head")
        self.far = (self.me + 2) % 4
        self.twin, self.across = head_neighbours()

    def copy(self, stage, at):
        member = self.far if stage == 2 else self.me
        cut = self.cuts(at)
        target = self.blocks.at[(member, *cut)]
        source = target if stage == 2 or self.own is None else self.own
        return remote(
            source,
            target,
            self.send.at[stage, at],
            self.receive.at[stage, at],
            self.across if stage == 0 else self.twin,
        )

    def start(self, at):
        self.copy(0, at).start()
        self.copy(1, at).start()

    def forward(self, at):
        self.copy(0, at).wait_recv()
        self.copy(2, at).start()

    def landed(self, at):
        self.copy(1, at).wait_recv()
        self.copy(2, at).wait_recv()

    def flush(self, at):
        for stage in range(3):
            self.copy(stage, at).wait_send()


class Pair:
    def __init__(self, half, at, size):
        self.size = size
        self.spans = [pl.ds(pl.multiple_of(start + at * size, size), size) for start in (0, half)]

    def load(self, ref):
        return jnp.concatenate([ref[span] for span in self.spans], 0)

    def store(self, ref, value):
        for number, span in enumerate(self.spans):
            ref[span] = value[number * self.size : (number + 1) * self.size]


def head_scratch(rows, columns):
    return [
        *[pltpu.VMEM((rows // 2, columns), jnp.bfloat16)] * 3,
        pltpu.SemaphoreType.DMA((3, CUT)),
        pltpu.SemaphoreType.DMA((3, CUT)),
    ]


def gather_scratch(number, count):
    return [
        pltpu.SemaphoreType.DMA((number, 2, count // 2)),
        pltpu.SemaphoreType.DMA((number, 2, count // 2)),
    ]


LIMIT = 60 * 2**20


def params(ident):
    return pltpu.CompilerParams(
        collective_id=ident, has_side_effects=True, vmem_limit_bytes=LIMIT
    )


VMEM = pl.BlockSpec(memory_space=pltpu.VMEM)
ANY = pl.BlockSpec(memory_space=pl.ANY)


def before_body(count, own, back, spans, state, outs, send, receive, spread_send, spread_receive, local):
    me = lax.axis_index("seq")
    column = lax.axis_index("head")
    greet((*head_neighbours(), *ring_neighbours(count)))
    source = back.at[:, :, : outs.shape[3]]
    keep = pltpu.make_async_copy(source, outs.at[column], local)
    keep.start()
    sharing = Spread(outs, source, lambda at: (), spread_send, spread_receive)
    spans[me] = own[...]
    ring = Gather(count, [(own, spans, (head,)) for head in range(own.shape[0])], send, receive)
    ring.advance(0)
    sharing.start(0)
    for step in range(1, ring.steps):
        ring.advance(step)
    ring.arrive(ring.steps - 1)
    heads = own.shape[0]

    def one(lap, states):
        moved = [
            mm(spans[lap, head, :, :DK], states[head])
            + spans[lap, head, :, DK:].astype(jnp.float32)
            for head in range(heads)
        ]
        return tuple(jnp.where(lap < me, new, old) for new, old in zip(moved, states))

    nothing = tuple(jnp.zeros((DK, DK), jnp.float32) for _ in range(heads))
    for head, result in enumerate(lax.fori_loop(0, count, one, nothing)):
        state[head] = result
    sharing.forward(0)
    sharing.landed(0)
    sharing.flush(0)
    keep.wait()
    ring.drain()


def states_before(own, back, count, ident):
    heads = own.shape[0]
    return pl.pallas_call(
        lambda *refs: before_body(count, *refs),
        out_shape=[
            jax.ShapeDtypeStruct((count, *own.shape), own.dtype),
            jax.ShapeDtypeStruct((heads, DK, DK), jnp.float32),
            jax.ShapeDtypeStruct((4, *back.shape[:2], heads * DK), back.dtype),
        ],
        in_specs=[VMEM, ANY],
        out_specs=[VMEM] * 3,
        scratch_shapes=[
            *gather_scratch(heads, count),
            pltpu.SemaphoreType.DMA((3, 1)),
            pltpu.SemaphoreType.DMA((3, 1)),
            pltpu.SemaphoreType.DMA,
        ],
        compiler_params=params(ident),
        name="states_before",
    )(own, back)


def after_body(count, own, spans, state, shifts, send, receive):
    me = lax.axis_index("seq")
    greet(ring_neighbours(count))
    shifts[me] = own[...]
    ring = Gather(count, [(own, shifts, (head,)) for head in range(own.shape[0])], send, receive)
    for step in range(ring.steps):
        ring.advance(step)
    ring.arrive(ring.steps - 1)
    heads = own.shape[0]

    def one(lap, states):
        source = count - 1 - lap
        moved = [
            tn(spans[source, head, :, :DK], states[head])
            + shifts[source, head].astype(jnp.float32)
            for head in range(heads)
        ]
        return tuple(jnp.where(source > me, new, old) for new, old in zip(moved, states))

    nothing = tuple(jnp.zeros((DK, DK), jnp.float32) for _ in range(heads))
    for head, result in enumerate(lax.fori_loop(0, count, one, nothing)):
        state[head] = result
    ring.drain()


def states_after(own, spans, count, ident):
    heads = own.shape[0]
    return pl.pallas_call(
        lambda *refs: after_body(count, *refs),
        out_shape=jax.ShapeDtypeStruct((heads, DK, DK), jnp.float32),
        in_specs=[VMEM] * 2,
        out_specs=VMEM,
        scratch_shapes=[
            pltpu.VMEM((count, *own.shape), own.dtype),
            *gather_scratch(heads, count),
        ],
        compiler_params=params(ident),
        name="states_after",
    )(own, spans)


def leave_body(
    count, members, heads, cuts, dx_hbm, tail_ref, dhist_ref, col_ref, normed_hbm, whole_hbm, tokens_hbm,
    middle_hbm, scales_ref, tiny_ref, ddecay_ref, expand_hbm, shrink_hbm, output_ref, summed_hbm, mlp_hbm,
    grad_ref, share_ref, tiny_share_ref, totals_ref, mlp_total_ref,
    work, parts, rim, part, total, near, half, far, hs, hr, near2, half2, far2, hs3, hr3,
    slots, staged, rs, rr,
    gains, tinies, tiny_slots, by_head, by_seq, ts, tr, hs2, hr2, ss2, sr2, rim_send, rim_receive,
    normed_ref, whole_ref, tokens_ref, middle_ref, expand_ref, shrink_ref, summed_ref, mlp_ref, loads,
):
    pairs = (
        (dx_hbm, work),
        (normed_hbm, normed_ref),
        (whole_hbm, whole_ref),
        (mlp_hbm, mlp_ref),
        (tokens_hbm, tokens_ref),
        (middle_hbm, middle_ref),
        (summed_hbm, summed_ref),
        (expand_hbm, expand_ref),
        (shrink_hbm, shrink_ref),
    )
    loading = [
        pltpu.make_async_copy(source, target, loads.at[number])
        for number, (source, target) in enumerate(pairs)
    ]
    for load in loading:
        load.start()
    row, column = lax.axis_index("seq"), lax.axis_index("head")
    head_peers = [{"head": (column + away) % members} for away in range(1, members)]
    span_peers = [{"seq": (row + away) % count} for away in range(1, count)]
    greet(head_peers + span_peers)
    back = remote(dhist_ref, rim, rim_send, rim_receive, {"seq": (row + count - 1) % count})
    back.start()
    length, model = tokens_ref.shape
    own_rows, columns = share_ref.shape
    full = (2 + 2 * NH) * DK
    width = (1 + 2 * NH) * DK
    seg_lane = (NH + 1) * heads
    back.wait_recv()
    loading[0].wait()
    end = col_ref[length - 8 :][7:8]
    for head in range(heads):
        lanes = slice(head * width, (head + 1) * width)
        returned = jnp.where(row < count - 1, rim[:, lanes], 0.0)
        place = lax.broadcasted_iota(jnp.int32, (8, width), 0)
        kept = jnp.where(place == 7, returned, 0.0)
        for distance in range(1, CONV - 1):
            flag = end[:, seg_lane + distance : seg_lane + distance + 1]
            kept = jnp.where(place == 7 - distance, returned * flag, kept)
        here = slice(head * full, head * full + width)
        before = work[length - 16 :, here].astype(jnp.float32)
        work[length - 16 :, here] = jnp.concatenate(
            [before[:8], tail_ref[:, lanes] + kept], 0
        ).astype(LOW)

    loading[1].wait()
    summing = HeadSum(part, total, near, half, far, hs, hr)
    outer = HeadSum(mlp_ref, mlp_total_ref, near2, half2, far2, hs3, hr3)
    ring = Scatter(count, (parts,), (slots,), (staged,), cuts, rs, rr)
    apart = own_rows % 128 == 0

    groups = (range(len(cuts) // 2), range(len(cuts) // 2, len(cuts)))

    def make(owner, way, group):
        for number, (which, start, size, direction) in enumerate(cuts):
            if direction == way and number in group:
                lanes = pl.ds(pl.multiple_of(owner * own_rows, own_rows), own_rows)
                parts[owner, :, start : start + size] = tn(
                    normed_ref[:, lanes], work[:, start : start + size]
                ).astype(LOW)

    def send(step, group):
        if apart:
            for way in range(2):
                make(ring.owner(step, way), way, group)
        ring.start(step, group)

    def make_own():
        if apart:
            for way in range(2):
                make(row, way, range(len(cuts)))

    if not apart:
        for owner in range(count):
            parts[owner] = tn(
                normed_ref[:, owner * own_rows : (owner + 1) * own_rows], work[...]
            ).astype(LOW)

    size = part.shape[0] // 2
    chunks = summed_ref.shape[0]
    gains[...] = jnp.zeros_like(gains)

    def norm_rows(span, incoming):
        values = tokens_ref[span].astype(jnp.float32)
        scale = lax.rsqrt(jnp.mean(values * values, -1, keepdims=True) + EPS_NORM)
        incoming = incoming.astype(jnp.float32)
        normal = values * scale
        scaled = incoming * scales_ref[0:1]
        inner = jnp.mean(normal * scaled, -1, keepdims=True)
        outgoing = middle_ref[span].astype(jnp.float32) + scale * (scaled - normal * inner)
        grad_ref[span] = outgoing.astype(LOW)
        gains[0:1] += jnp.sum(incoming * normal, 0, keepdims=True)

    def norm_chunk(chunk):
        norm_rows(slice((chunks - chunk) * size, (chunks - chunk + 1) * size), summed_ref[chunk])

    ends = (slice(length - size, length), slice(0, size))

    def part_rows(number):
        part[number * size : (number + 1) * size] = nt(
            work[ends[number]], whole_ref[...].reshape(model, columns)
        ).astype(LOW)

    def end_rows(number):
        norm_rows(ends[number], total[number * size : (number + 1) * size])

    def run(*items):
        return lambda: [item() for item in items]

    late = ring.steps - 1
    norms = [lambda chunk=chunk: norm_chunk(chunk) for chunk in range(chunks)]
    queue = [
        run(loading[2].wait, lambda: part_rows(0)),
        run(lambda: part_rows(1), summing.first),
        run(summing.second, loading[3].wait, outer.first),
        make_own,
        outer.second,
        run(*[load.wait for load in loading[4:]], norms[0]),
        norms[1],
        summing.third,
        norms[2],
        run(summing.landed, lambda: end_rows(0)),
        lambda: end_rows(1),
        norms[3],
        lambda: outer.third(range(CUT // 2)),
        run(*norms[4:]),
    ]
    for step in range(late + 1):
        for number, group in enumerate(groups):
            send(step, group)
            at = 2 * step + number
            if at < len(queue):
                queue[at]()
    for owner in range(count):
        tinies[owner] = tiny_ref[owner]
        tinies[owner, heads : heads + 1, :own_rows] = gains[
            0:1, owner * own_rows : (owner + 1) * own_rows
        ]
    tiny_slots[row] = tinies[row]
    sends = []
    for away, device in enumerate(span_peers):
        copy = remote(
            tinies.at[(row + away + 1) % count], tiny_slots.at[row], ts.at[away], tr.at[away], device
        )
        copy.start()
        sends.append(copy)

    def square_sum(values):
        return jnp.sum(jnp.sum(values * values, 0, keepdims=True), 1, keepdims=True)

    squares = square_sum(expand_ref[...]) + square_sum(shrink_ref[...]) + square_sum(output_ref[...])
    outer.third(range(CUT // 2, CUT))
    ring.finish((share_ref,))
    squares = squares + square_sum(share_ref[...])
    for copy in sends:
        copy.wait_recv()
    tiny_share = jnp.sum(tiny_slots[...], 0)
    tiny_share_ref[...] = tiny_share
    rows16 = lax.broadcasted_iota(jnp.int32, tiny_share.shape, 0)
    weight = jnp.where((rows16 >= heads) & (rows16 < heads + 2), members**-0.5, 1.0)
    squares = squares + square_sum(tiny_share * weight)
    places = lax.broadcasted_iota(jnp.int32, (8, 128), 0)
    lanes = lax.broadcasted_iota(jnp.int32, (8, 128), 1)
    tile_value = jnp.where((places == 2) & (lanes == 0), squares, 0.0)
    for head in range(heads):
        at = (NH + 1) * head + NH
        value = ddecay_ref[:, at : at + 1]
        tile_value = jnp.where((places < 2) & (lanes == column * heads + head), value, tile_value)
    by_head[column] = tile_value
    copies = [
        remote(by_head.at[column], by_head.at[column], hs2.at[away], hr2.at[away], device)
        for away, device in enumerate(head_peers)
    ]
    for copy in copies:
        copy.start()
    for copy in copies:
        copy.wait_recv()
    by_seq[row] = jnp.sum(by_head[...], 0)
    later = [
        remote(by_seq.at[row], by_seq.at[row], ss2.at[away], sr2.at[away], device)
        for away, device in enumerate(span_peers)
    ]
    for copy in later:
        copy.start()
    for copy in later:
        copy.wait_recv()
    totals_ref[...] = jnp.sum(by_seq[...], 0)
    summing.flush()
    outer.finish()
    for copy in [back] + sends + copies + later:
        copy.wait_send()


def leave(
    dx, tail, dhistory, col, normed, whole, tokens, middle, scales, tiny, ddecay, expand, shrink, output,
    summed, mlp, heads, ident,
):
    length, model = tokens.shape
    count, own_rows, width = whole.shape
    members = lax.axis_size("head")
    f32 = jnp.float32
    dma = pltpu.SemaphoreType.DMA
    parts = 4
    rest = 2 * summed.shape[1]
    return pl.pallas_call(
        lambda *refs: leave_body(count, members, heads, scatter_cuts([width], [parts]), *refs),
        out_shape=[
            jax.ShapeDtypeStruct(tokens.shape, LOW),
            jax.ShapeDtypeStruct((own_rows, width), f32),
            jax.ShapeDtypeStruct(tiny.shape[1:], f32),
            jax.ShapeDtypeStruct((8, 128), f32),
            jax.ShapeDtypeStruct(mlp.shape, LOW),
        ],
        in_specs=[
            ANY, VMEM, VMEM, VMEM, ANY, ANY, ANY, ANY, VMEM, VMEM, VMEM, ANY, ANY, VMEM, ANY, ANY,
        ],
        out_specs=[VMEM] * 5,
        scratch_shapes=[
            pltpu.VMEM(dx.shape, LOW),
            pltpu.VMEM((count, own_rows, width), LOW),
            pltpu.VMEM(dhistory.shape, f32),
            pltpu.VMEM((rest, model), LOW),
            pltpu.VMEM((rest, model), LOW),
            *head_scratch(rest, model),
            *head_scratch(length, model),
            *scatter_scratch(count, [own_rows], [width], [parts]),
            pltpu.VMEM((8, model), f32),
            pltpu.VMEM(tiny.shape, f32),
            pltpu.VMEM(tiny.shape, f32),
            pltpu.VMEM((members, 8, 128), f32),
            pltpu.VMEM((count, 8, 128), f32),
            *[dma((count - 1,))] * 2,
            *[dma((members - 1,))] * 2,
            *[dma((count - 1,))] * 2,
            *[dma] * 2,
            *[
                pltpu.VMEM(array.shape, array.dtype)
                for array in (normed, whole, tokens, middle, expand, shrink, summed, mlp)
            ],
            dma((9,)),
        ],
        compiler_params=params(ident),
        name="leave",
    )(
        dx, tail, dhistory, col, normed, whole, tokens, middle, scales, tiny, ddecay, expand, shrink,
        output, summed, mlp,
    )


def update_body(sizes, *refs):
    heads, units, coeff_count, kernel_columns, own_rows, gating_columns = sizes
    mixer, expand, shrink, output, tiny, totals, tokens, mixed, mlp = refs[:9]
    olds, news = refs[9:36], refs[36:]
    news[34][...] = (
        tokens[...].astype(jnp.float32)
        + mixed[...].astype(jnp.float32)
        + mlp[...].astype(jnp.float32)
    ).astype(LOW)
    columns = olds[0].shape[1]
    padded = shrink.shape[1]
    decay_grad = totals[0:2, :H]
    norm = jnp.sqrt(
        totals[2:3, 0:1]
        + jnp.sum(jnp.sum(decay_grad * decay_grad, 0, keepdims=True), 1, keepdims=True)
    )
    factor = jnp.minimum(1.0, CLIP_NORM / (norm + 1e-06))
    news[33][...] = jnp.broadcast_to(norm, (8, 128))
    grads = (
        lambda: mixer[:, :columns],
        lambda: mixer[:, columns:].T[:coeff_count],
        lambda: tiny[:heads, :kernel_columns],
        lambda: output[...].T,
        None,
        lambda: shrink[...].T[:units],
        lambda: tiny[heads : heads + 2, :own_rows],
        lambda: tiny[heads + 2 : 2 * heads + 2, :gating_columns],
        lambda: decay_grad,
    )
    rates = (LEARN_RATE,) * 2 + (KERNEL_RATE,) + (LEARN_RATE,) * 3 + (GAIN_RATE,) * 2 + (DECAY_RATE,)
    at = 0
    for number, grad in enumerate(grads):
        weight, first, second = olds[3 * number : 3 * number + 3]
        copied = number < 6
        outs = news[at : at + 3 + copied]
        at += 3 + copied
        places = [...]
        if number == 4:
            places = [0, 1]
        for half, place in enumerate(places):
            if number == 4:
                gradient = expand[:, half * padded : (half + 1) * padded].T[:units]
            else:
                gradient = grad()
            found = adamw(
                weight[place], first[place], second[place], gradient, factor, rates[number],
                WEIGHT_DECAY if copied else 0.0,
            )
            for out, value in zip(outs, found):
                out[place] = value
            if copied:
                outs[3][place] = found[0].astype(LOW)


def update(shares, olds, sizes):
    f32 = jnp.float32
    shapes = []
    for number in range(9):
        shape = olds[3 * number].shape
        shapes += [jax.ShapeDtypeStruct(shape, f32)] * 3
        if number < 6:
            shapes.append(jax.ShapeDtypeStruct(shape, LOW))
    shapes.append(jax.ShapeDtypeStruct((8, 128), f32))
    shapes.append(jax.ShapeDtypeStruct(shares[-1].shape, LOW))
    return pl.pallas_call(
        lambda *refs: update_body(sizes, *refs),
        out_shape=shapes,
        in_specs=[VMEM] * (len(shares) + len(olds)),
        out_specs=[VMEM] * len(shapes),
        compiler_params=pltpu.CompilerParams(vmem_limit_bytes=LIMIT),
        name="update",
    )(*shares, *olds)


def block_triangle(size):
    row_ids = lax.broadcasted_iota(jnp.int32, (size, size), 0)
    col_ids = lax.broadcasted_iota(jnp.int32, (size, size), 1)
    same = row_ids // STRETCH == col_ids // STRETCH
    return (same & (row_ids >= col_ids)).astype(jnp.float32)


def exact(left, right, dims):
    return lax.dot_general(
        left,
        right,
        (dims, ((), ())),
        precision=lax.Precision.HIGHEST,
        preferred_element_type=jnp.float32,
    )


def decay_terms(coeff, decay):
    shifted = coeff + decay[1:2]
    return jnp.maximum(shifted, 0.0) + jnp.log1p(jnp.exp(-jnp.abs(shifted))), shifted


def enter_body(
    count, heads, project_ref, coeffs_ref, kernel_ref, gains_ref, gating_ref, output_ref, shrink_ref,
    expand_ref, decays_ref, tokens_ref, starts_ref,
    whole_ref, tinies_ref, normed_ref, projected_ref, coeff_ref, col_ref, row_ref, hist_ref,
    back_ref, rest_ref, decay_ref,
    own_ref, tiny_ref, tiny_wide, acc, root, marks, rim_out, rim_in, send, receive, rim_send, rim_receive,
):
    length, model = tokens_ref.shape
    rows, columns = project_ref.shape
    full = (2 + 2 * NH) * DK
    width = (1 + 2 * NH) * DK
    tile = 256
    me = lax.axis_index("seq")
    following = {"seq": (me + 1) % count}
    previous = {"seq": (me + count - 1) % count}
    own_ref[:, :columns] = project_ref[...].astype(LOW)
    coeff_count = coeffs_ref.shape[0]
    own_ref[:, columns:] = jnp.concatenate(
        [coeffs_ref[...], jnp.zeros((128 - coeff_count, rows), jnp.float32)], 0
    ).T.astype(LOW)
    tiny_wide[...] = jnp.zeros_like(tiny_wide)
    tiny_wide[:heads, : kernel_ref.shape[1]] = kernel_ref[...]
    tiny_wide[heads : heads + 2, :rows] = gains_ref[...]
    tiny_wide[heads + 2 : 2 * heads + 2, : gating_ref.shape[1]] = gating_ref[...]
    tiny_ref[...] = tiny_wide[...].astype(LOW)
    whole_ref[me] = own_ref[...]
    tinies_ref[me] = tiny_ref[...]
    greet((*ring_neighbours(count), following, previous))
    items = pieces(own_ref, whole_ref, 4) + [(tiny_ref, tinies_ref, (slice(None),) * 2)]
    ring = Gather(count, items, send, receive)
    ring.advance(0)

    lane8 = lax.broadcasted_iota(jnp.int32, (8, 128), 1)
    place8 = lax.broadcasted_iota(jnp.int32, (8, 128), 0)
    decays = decays_ref[...].astype(LOW).astype(jnp.float32)
    head_lane = lax.broadcasted_iota(jnp.int32, decays.shape, 1)
    table = jnp.zeros((8, 128), jnp.float32)
    for head in range(heads):
        chosen = head_lane == lax.axis_index("head") * heads + head
        found = jnp.sum(jnp.where(chosen, decays, 0.0), -1, keepdims=True)
        lane_here = lane8 == (NH + 1) * head + NH
        table = jnp.where(lane_here & (place8 == 0), jnp.exp(found[0:1]), table)
        table = jnp.where(lane_here & (place8 == 1), found[1:2], table)
    decay_ref[...] = table

    def measure(at, nothing):
        span = pl.ds(at * tile, tile)
        values = tokens_ref[span].astype(jnp.float32)
        scale = lax.rsqrt(jnp.mean(values * values, -1, keepdims=True) + EPS_NORM)
        root[span] = jnp.broadcast_to(scale, (tile, 128))
        return nothing

    lax.fori_loop(0, length // tile, measure, 0)

    def add(origins, first):
        def one(at, nothing):
            span = pl.ds(at * tile, tile)
            scale = root[span][:, :1]
            pieces = []
            for origin in origins:
                lanes = pl.ds(pl.multiple_of(origin * rows, rows), rows)
                gains = tinies_ref[origin, :, :rows].astype(jnp.float32)[2:3]
                piece = (tokens_ref[span, lanes].astype(jnp.float32) * scale * gains).astype(LOW)
                normed_ref[span, lanes] = piece
                pieces.append(piece)
            left = pieces[0] if len(pieces) == 1 else jnp.concatenate(pieces, 1)
            right = [whole_ref[origin] for origin in origins]
            right = right[0] if len(right) == 1 else jnp.concatenate(right, 0)
            moved = mm(left, right)
            acc[span] = moved if first else acc[span] + moved
            return nothing

        lax.fori_loop(0, length // tile, one, 0)

    apart = rows % 128 == 0
    if apart:
        add([me], True)
    units = shrink_ref.shape[0]
    mixer_rows = output_ref.shape[0]
    early = back_ref.shape[1] + rest_ref.shape[1] - mixer_rows
    padded = early // 3
    early = back_ref.shape[1] - mixer_rows - padded
    blank = jnp.zeros((rows, padded - units), LOW)
    back_ref[:, :mixer_rows] = output_ref[...].T.astype(LOW)
    back_ref[:, mixer_rows : mixer_rows + padded] = jnp.concatenate(
        [shrink_ref[...].T.astype(LOW), blank], 1
    )
    gate = jnp.concatenate([expand_ref[0].T.astype(LOW), blank], 1)
    back_ref[:, mixer_rows + padded :] = gate[:, :early]
    rest_ref[:, : padded - early] = gate[:, early:]
    rest_ref[:, padded - early :] = jnp.concatenate([expand_ref[1].T.astype(LOW), blank], 1)

    lane = lax.broadcasted_iota(jnp.int32, (128, 128), 1)
    eye = (lane == lax.broadcasted_iota(jnp.int32, (128, 128), 0)).astype(jnp.float32)
    seg_lane = (NH + 1) * heads
    marks[:8] = jnp.zeros((8, 128), jnp.float32)
    for group in range(length // 128):
        line = jnp.broadcast_to(starts_ref[group : group + 1].astype(jnp.float32), (128, 128))
        marks[8 + 128 * group : 8 + 128 * (group + 1)] = jnp.broadcast_to(
            jnp.sum(line * eye, -1, keepdims=True), (128, 128)
        )

    for step in range(ring.steps):
        if step + 1 < ring.steps:
            ring.advance(step + 1)
        else:
            ring.arrive(step)
        if apart:
            add([ring.origin(step + 1, way) for way in range(2 if step + 1 < ring.steps else 1)], False)
    if not apart:
        gains = jnp.concatenate(
            [tinies_ref[origin, :, :rows].astype(jnp.float32)[2:3] for origin in range(count)], 1
        )

        def at_once(at, nothing):
            span = pl.ds(at * tile, tile)
            values = tokens_ref[span].astype(jnp.float32) * root[span][:, :1] * gains
            normed_ref[span] = values.astype(LOW)
            acc[span] = mm(values, whole_ref[...].reshape(model, columns + 128))
            return nothing

        lax.fori_loop(0, length // tile, at_once, 0)

    rim_out[...] = jnp.zeros_like(rim_out)
    flag = jnp.ones((1, 1), jnp.float32)
    flags = []
    for back in range(CONV - 2):
        flag = flag * (1.0 - marks[8 + length - 1 - back : 8 + length - back, :1])
        flags.append(flag)
    for head in range(heads):
        last_rows = acc[length - 16 :, head * full : head * full + width].astype(LOW).astype(
            jnp.float32
        )
        place = lax.broadcasted_iota(jnp.int32, (16, width), 0)
        kept = jnp.where(place == 15, last_rows, 0.0)
        for back in range(1, CONV - 1):
            kept = jnp.where(place == 15 - back, last_rows * flags[back - 1], kept)
        rim_out[:, head * width : (head + 1) * width] = kept.astype(LOW)
    rim = remote(rim_out, rim_in, rim_send, rim_receive, following)
    rim.start()

    triangle = block_triangle(128)
    rate_lane = (lane < seg_lane) & (lane % (NH + 1) == NH)
    for group in range(length // 128):
        span = slice(128 * group, 128 * (group + 1))
        at = 8 + 128 * group
        projected_ref[span] = acc[span, :columns].astype(LOW)
        coeff_low = acc[span, columns:].astype(LOW)
        coeff_ref[span] = coeff_low
        coeff = coeff_low.astype(jnp.float32)
        soft, unused = decay_terms(coeff, decay_ref[...])
        begins = marks[at : at + 128]
        logs = jnp.where(rate_lane, -decay_ref[0:1] * soft, 0.0)
        logs = jnp.where(lane == seg_lane, begins, logs)
        summed = exact(triangle, logs, ((1,), (0,)))
        linked = 1.0 - begins
        table = jnp.where(
            rate_lane | (lane == seg_lane), summed, 1.0 / (1.0 + jnp.exp(-(coeff + STEP_OFFSET)))
        )
        for back in range(1, CONV):
            if back > 1:
                linked = linked * (1.0 - marks[at - back + 1 : at - back + 129])
            table = jnp.where(lane == seg_lane + back, linked, table)
        col_ref[span] = table
        flipped = table.T[:16]
        swapped = pltpu.roll(flipped, STRETCH, 1)
        low_lanes = lax.broadcasted_iota(jnp.int32, (16, 128), 1) < STRETCH
        row_ref[2 * group] = jnp.where(low_lanes, flipped, swapped)
        row_ref[2 * group + 1] = jnp.where(low_lanes, swapped, flipped)

    rim.wait_recv()
    hist_ref[...] = jnp.where(me > 0, rim_in[...].astype(jnp.float32)[8:], 0.0)
    rim.wait_send()
    ring.drain()


EARLY = 512


def enter(
    project, coeffs, kernel, gains, gating, output, shrink, expand, decays, tokens, starts, count, heads,
    padded, tiny_columns, ident,
):
    length, model = tokens.shape
    rows, columns = project.shape
    width = (1 + 2 * NH) * DK
    f32 = jnp.float32
    return pl.pallas_call(
        lambda *refs: enter_body(count, heads, *refs),
        out_shape=[
            jax.ShapeDtypeStruct((count, rows, columns + 128), LOW),
            jax.ShapeDtypeStruct((count, 16, tiny_columns), LOW),
            jax.ShapeDtypeStruct((length, model), LOW),
            jax.ShapeDtypeStruct((length, columns), LOW),
            jax.ShapeDtypeStruct((length, 128), LOW),
            jax.ShapeDtypeStruct((length, 128), f32),
            jax.ShapeDtypeStruct((length // STRETCH, 16, 128), f32),
            jax.ShapeDtypeStruct((8, heads * width), f32),
            jax.ShapeDtypeStruct((rows, output.shape[0] + padded + EARLY), LOW),
            jax.ShapeDtypeStruct((rows, 2 * padded - EARLY), LOW),
            jax.ShapeDtypeStruct((8, 128), f32),
        ],
        in_specs=[VMEM] * 11,
        out_specs=[VMEM] * 11,
        scratch_shapes=[
            pltpu.VMEM((rows, columns + 128), LOW),
            pltpu.VMEM((16, tiny_columns), LOW),
            pltpu.VMEM((16, tiny_columns), f32),
            pltpu.VMEM((length, columns + 128), f32),
            pltpu.VMEM((length, 128), f32),
            pltpu.VMEM((8 + length, 128), f32),
            pltpu.VMEM((16, heads * width), LOW),
            pltpu.VMEM((16, heads * width), LOW),
            *gather_scratch(5, count),
            pltpu.SemaphoreType.DMA,
            pltpu.SemaphoreType.DMA,
        ],
        compiler_params=params(ident),
        name="enter",
    )(project, coeffs, kernel, gains, gating, output, shrink, expand, decays, tokens, starts)


SUB = 2
LEVELS = 7
LOW = jnp.bfloat16
GONE = -1e30


def contract(left, right, dims):
    return lax.dot_general(
        left.astype(LOW), right.astype(LOW), (dims, ((), ())), preferred_element_type=jnp.float32
    )


def mm(left, right):
    return contract(left, right, ((1,), (0,)))


def nt(left, right):
    return contract(left, right, ((1,), (1,)))


def tn(left, right):
    return contract(left, right, ((0,), (0,)))


def block_masks():
    steps = NH * STRETCH
    place = np.arange(steps)
    token, step = place % STRETCH, place // STRETCH
    row_token, col_token = token[:, None], token[None, :]
    row_step, col_step = step[:, None], step[None, :]
    masks = [(row_token == col_token) & (row_step > col_step)]
    size = 1
    while size < STRETCH:
        masks.append(
            (row_token // (2 * size) == col_token // (2 * size))
            & (row_token // size == col_token // size + 1)
        )
        size *= 2
    masks.append((row_token > col_token) | masks[0])
    masks.append(row_token >= col_token)
    return np.stack(masks).astype(np.float32)


def chain_scalars(col, row, head, rows, heads):
    base = (NH + 1) * head
    seg_lane = (NH + 1) * heads

    def twice(lane):
        part = col[rows, lane : lane + 1]
        return jnp.concatenate([part] * NH, 0)

    cum_col, seg_col = twice(base + NH), twice(seg_lane)
    beta_col = jnp.concatenate([col[rows, base + j : base + j + 1] for j in range(NH)], 0)
    cum_row, seg_row = row[base + NH : base + NH + 1], row[seg_lane : seg_lane + 1]
    cum_end = cum_row[:, STRETCH - 1 : STRETCH]
    seg_end = seg_row[:, STRETCH - 1 : STRETCH]
    initial = jnp.where(seg_col == 0.0, jnp.exp(cum_col), 0.0)
    last = jnp.exp(jnp.where(seg_col == seg_end, cum_end - cum_col, GONE))
    keep = jnp.where(seg_end == 0.0, jnp.exp(cum_end), 0.0)
    return cum_col, seg_col, beta_col, cum_row, seg_row, initial, last, keep


def retained(cum_col, seg_col, cum_row, seg_row, reach):
    valid = (seg_col == seg_row) & (reach > 0.0)
    return jnp.exp(jnp.where(valid, cum_col - cum_row, GONE))


def silu_parts(values):
    gate = 1.0 / (1.0 + jnp.exp(-values))
    return values * gate, gate * (1.0 + values * (1.0 - gate))


def head_values(activated, rows):
    queries = activated[rows, :DK]
    keys, scales = [], []
    for j in range(NH):
        part = activated[rows, (1 + j) * DK : (2 + j) * DK]
        scale = lax.rsqrt(jnp.sum(part * part, -1, keepdims=True) + EPS_KEY)
        keys.append(part * scale)
        scales.append(scale)
    values = [activated[rows, (1 + NH + j) * DK : (2 + NH + j) * DK] for j in range(NH)]
    return queries, jnp.concatenate(keys, 0), jnp.concatenate(values, 0), jnp.concatenate(scales, 0)


def along_grid(step, grid, total, run, late=0):
    share = -(-total // grid)
    apart = max(1, grid // total)
    late = min(late, apart - 1)
    for number, begin in enumerate(range(0, total, share)):

        @pl.when(step == number * apart + late)
        def _():
            for one in range(begin, min(begin + share, total)):
                run(one)


def forward_body(
    steps_here, count, heads, x_ref, hist_ref, taps_ref, col_ref, row_ref, mask_ref, own_ref,
    pre_ref, t_ref, uw_ref, aug_ref, delta_ref, score_ref, qk_ref, fo_ref, span_ref, whole_ref,
    line, carry, send, receive, local,
):
    seg_lane = (NH + 1) * heads
    width = (1 + 2 * NH) * DK
    full = (2 + 2 * NH) * DK
    step = pl.program_id(0)
    length = x_ref.shape[0]
    grid = pl.num_programs(0)
    ring = Gather(count, pieces(own_ref, whole_ref, 4), send, receive)
    me = lax.axis_index("seq")
    keeps = [pltpu.make_async_copy(own_ref, whole_ref.at[me], local)]

    @pl.when(step == 0)
    def _():
        greet(ring_neighbours(count))
        for keep in keeps:
            keep.start()

    along_grid(step, steps_here, ring.steps, lambda number: ring.advance(number, (0, 1)))
    along_grid(step, steps_here, ring.steps, lambda number: ring.advance(number, (2, 3)), 1)

    @pl.when(step == 0)
    def _():
        line[:8] = hist_ref[...]
        ones = (
            lax.broadcasted_iota(jnp.int32, (DK, 2 * DK), 0)
            == lax.broadcasted_iota(jnp.int32, (DK, 2 * DK), 1)
        ).astype(jnp.float32)
        for head in range(heads):
            carry[head] = ones

    col = col_ref[...]
    activated = []
    for head in range(heads):
        lanes = slice(head * width, (head + 1) * width)
        line[8:, lanes] = x_ref[:, head * full : head * full + width].astype(jnp.float32)
        total = line[8:, lanes] * taps_ref[CONV - 1 : CONV, lanes]
        for back in range(1, CONV):
            shifted = line[8 - back : 8 - back + length, lanes]
            kept = jnp.where(col[:, seg_lane + back : seg_lane + back + 1] > 0.0, shifted, 0.0)
            total = total + kept * taps_ref[CONV - 1 - back : CONV - back, lanes]
        pre_ref[:, lanes] = total
        activated.append(silu_parts(total)[0])
    line[:8] = line[length:]

    chains = [(head, sub) for sub in range(SUB) for head in range(heads)]
    work = {}
    strict, reach = mask_ref[LEVELS], mask_ref[LEVELS + 1]
    for head, sub in chains:
        rows = slice(sub * STRETCH, (sub + 1) * STRETCH)
        queries, keys, values, unused = head_values(activated[head], rows)
        cum_col, seg_col, beta, cum_row, seg_row, initial, last, keep = chain_scalars(
            col, row_ref[sub], head, rows, heads
        )
        kept = retained(cum_col, seg_col, cum_row, seg_row, reach)
        gram = nt(jnp.concatenate([queries, keys], 0), keys)
        lower = beta * kept * gram[STRETCH:] * strict
        score = gram[:STRETCH] * kept[:STRETCH]
        ones = (
            lax.broadcasted_iota(jnp.int32, lower.shape, 0)
            == lax.broadcasted_iota(jnp.int32, lower.shape, 1)
        ).astype(jnp.float32)
        work[head, sub] = dict(
            lower=lower, solved=ones - lower * mask_ref[0], score=score, queries=queries, keys=keys,
            right=jnp.concatenate([beta * values, (beta * initial) * keys], 1),
            initial=initial, last=last, keep=keep,
        )
        score_ref[head, sub] = score.astype(LOW)
        qk_ref[head, sub, :STRETCH] = queries.astype(LOW)
        qk_ref[head, sub, STRETCH:] = keys.astype(LOW)
    for level in range(1, LEVELS):
        below = {c: mm(work[c]["lower"] * mask_ref[level], work[c]["solved"]) for c in chains}
        for c in chains:
            work[c]["solved"] = work[c]["solved"] - mm(work[c]["solved"], below[c])
    for c in chains:
        work[c]["uw"] = mm(work[c]["solved"], work[c]["right"])
        t_ref[c[0], c[1]] = work[c]["solved"].astype(LOW)
        uw_ref[c[0], c[1]] = work[c]["uw"].astype(LOW)
    for c in chains:
        head, sub = c
        one = work[c]
        state = carry[head]
        aug_ref[head, sub] = state.astype(LOW)
        read = mm(
            jnp.concatenate([one["queries"] * one["initial"][:STRETCH], one["uw"][:, DK:]], 0), state
        )
        delta = jnp.concatenate(
            [-read[STRETCH:, :DK], one["uw"][:, :DK] - read[STRETCH:, DK:]], 1
        )
        delta_ref[head, sub] = delta.astype(LOW)
        carry[head] = one["keep"] * state + tn(one["keys"] * one["last"], delta)
        fo_ref[head, sub * STRETCH : (sub + 1) * STRETCH] = read[:STRETCH] + mm(one["score"], delta)
    span_ref[...] = carry[...].astype(LOW)

    @pl.when(step == grid - 1)
    def _():
        ring.arrive(ring.steps - 1)
        ring.drain()
        for keep in keeps:
            keep.wait()


def block_spec(shape, axis, count=None):
    def index(step):
        place = step if count is None else count - 1 - step
        return tuple(place if i == axis else 0 for i in range(len(shape)))

    return pl.BlockSpec(shape, index)


def whole_spec(shape):
    return pl.BlockSpec(shape, lambda step: (0,) * len(shape))


def mixer_forward(projected, history, taps, col, row, masks, own, heads, count, ident):
    length = projected.shape[0]
    blocks = length // STRETCH
    grid = blocks // SUB
    rows = SUB * STRETCH
    steps = NH * STRETCH
    conv = history.shape[1]
    f32 = jnp.float32
    shapes = [
        ((length, conv), f32, (rows, conv), 0),
        ((heads, blocks, steps, steps), LOW, (heads, SUB, steps, steps), 1),
        ((heads, blocks, steps, 2 * DK), LOW, (heads, SUB, steps, 2 * DK), 1),
        ((heads, blocks, DK, 2 * DK), LOW, (heads, SUB, DK, 2 * DK), 1),
        ((heads, blocks, steps, 2 * DK), LOW, (heads, SUB, steps, 2 * DK), 1),
        ((heads, blocks, STRETCH, steps), LOW, (heads, SUB, STRETCH, steps), 1),
        ((heads, blocks, STRETCH + steps, DK), LOW, (heads, SUB, STRETCH + steps, DK), 1),
        ((heads, length, 2 * DK), f32, (heads, rows, 2 * DK), 1),
        ((heads, DK, 2 * DK), LOW, (heads, DK, 2 * DK), None),
    ]
    return pl.pallas_call(
        lambda *refs: forward_body(grid, count, heads, *refs),
        grid=(grid,),
        out_shape=[
            *[jax.ShapeDtypeStruct(s[0], s[1]) for s in shapes],
            jax.ShapeDtypeStruct((count, *own.shape), own.dtype),
        ],
        in_specs=[
            block_spec((rows, projected.shape[1]), 0),
            whole_spec(history.shape),
            whole_spec(taps.shape),
            block_spec((rows, 128), 0),
            block_spec((SUB, *row.shape[1:]), 0),
            whole_spec(masks.shape),
            ANY,
        ],
        out_specs=[
            *[whole_spec(s[2]) if s[3] is None else block_spec(s[2], s[3]) for s in shapes],
            ANY,
        ],
        scratch_shapes=[
            pltpu.VMEM((8 + rows, conv), f32),
            pltpu.VMEM((heads, DK, 2 * DK), f32),
            *gather_scratch(4, count),
            pltpu.SemaphoreType.DMA,
        ],
        compiler_params=params(ident),
        name="mixer_forward",
    )(projected, history, taps, col, row, masks, own)


def feed_body(
    count, heads, cuts_of, fo_ref, state_ref, x_ref, gating_ref, back_hbm, outs_hbm, own_ref, tokens_hbm,
    cot_hbm, scales_ref,
    res_ref, mixed_ref, mlp_ref, grad_ref, expand_ref, shrink_share, output_ref, gain_ref,
    gated_all, whole, part2, total2, near2, half2, far2, s2, r2, shrink_parts, hidden, opened, second,
    incoming, gs, gr, spread_send, spread_receive, slots, staged, rs, rr,
    back_ref, outs_ref, tokens_ref, cot_ref, loads,
):
    pairs = (
        (back_hbm, back_ref), (cot_hbm, cot_ref), (outs_hbm, outs_ref), (tokens_hbm, tokens_ref)
    )
    loading = [
        pltpu.make_async_copy(source, target, loads.at[number])
        for number, (source, target) in enumerate(pairs)
    ]
    for load in loading:
        load.start()
    full = (2 + 2 * NH) * DK
    mixer_rows = heads * DK
    length, model = tokens_ref.shape
    own_rows = own_ref.shape[0]
    units = hidden.shape[1]
    early = back_ref.shape[2] - mixer_rows - units
    greet((*head_neighbours(), *ring_neighbours(count)))
    whole[lax.axis_index("seq")] = own_ref[...]
    ring = Gather(count, pieces(own_ref, whole, 4), gs, gr)
    ring.advance(0)
    two = HeadSum(part2, total2, near2, half2, far2, s2, r2)
    scatter = Scatter(count, (shrink_parts,), (slots,), (staged,), cuts_of, rs, rr)
    size = length // 8
    steps = 4
    column = lax.axis_index("head")
    sharing = Spread(
        gated_all,
        None,
        lambda at: (pl.ds(pl.multiple_of(at * size, size), size),),
        spread_send,
        spread_receive,
    )
    each = CUT // steps

    def cuts(at):
        return [at * each + number for number in range(each)]

    def columns(ref, start, stop):
        return ref[:, :, start:stop].reshape(model, stop - start)

    def finish_rows(at):
        span = pl.ds(pl.multiple_of(at * size, size), size)
        parts = []
        for head in range(heads):
            result = fo_ref[head, span, DK:] + mm(fo_ref[head, span, :DK], state_ref[head])
            res_ref[head, span] = result
            scale = lax.rsqrt(jnp.mean(result * result, -1, keepdims=True) + EPS_NORM)
            gate = x_ref[span, (head + 1) * full - DK : (head + 1) * full].astype(jnp.float32)
            parts.append(result * scale * gating_ref[head : head + 1] * silu_parts(gate)[0])
        gated_all[column, span] = jnp.concatenate(parts, 1).astype(LOW)
        sharing.start(at)

    def hidden_grads(at, nothing):
        span = pl.ds(pl.multiple_of(at * 256, 256), 256)
        incoming[span] = mm(cot_ref[span], columns(back_ref, mixer_rows, mixer_rows + units))
        return nothing

    for at in range(steps):
        finish_rows(at)
        finish_rows(at + steps)
        if at == 2:
            ring.advance(1)
    for load in loading:
        load.wait()
    lax.fori_loop(0, length // 256, hidden_grads, 0)
    for step in range(2, ring.steps):
        ring.advance(step)
        if step == 2:
            for at in range(steps):
                sharing.forward(at)
                sharing.forward(at + steps)
    ring.arrive(ring.steps - 1)

    def feed_rows(at, nothing):
        sharing.landed(at)
        sharing.landed(at + steps)
        rows = Pair(length // 2, at, size)
        mixed = jnp.zeros((2 * size, model), jnp.float32)
        for member in range(4):
            mixed = mixed + nt(
                rows.load(gated_all.at[member]), outs_ref[member].reshape(model, mixer_rows)
            )
        mixed = mixed.astype(LOW)
        rows.store(mixed_ref, mixed)
        middle = rows.load(tokens_ref).astype(jnp.float32) + mixed.astype(jnp.float32)
        scale = lax.rsqrt(jnp.mean(middle * middle, -1, keepdims=True) + EPS_NORM)
        normal = (middle * scale * scales_ref[0:1]).astype(LOW)
        rows.store(second, normal)
        gate = jnp.concatenate(
            [
                mm(normal, columns(back_ref, mixer_rows + units, mixer_rows + units + early)),
                mm(normal, columns(whole, 0, units - early)),
            ],
            1,
        )
        up = mm(normal, columns(whole, units - early, 2 * units - early))
        active, slope = silu_parts(gate)
        product = (active * up).astype(LOW)
        rows.store(hidden, product)
        grad_hidden = rows.load(incoming)
        grad_gate = (grad_hidden * up * slope).astype(LOW)
        grad_up = (grad_hidden * active).astype(LOW)
        grads = jnp.concatenate([grad_gate, grad_up], 1)
        rows.store(opened, grads)
        rows.store(
            part2,
            (
                nt(
                    grad_gate[:, :early],
                    columns(back_ref, mixer_rows + units, mixer_rows + units + early),
                )
                + nt(grads[:, early:], columns(whole, 0, 2 * units - early))
            ).astype(LOW),
        )
        two.first(cuts(at))

        @pl.when(at > 0)
        def _():
            two.second(cuts(at - 1))

        return nothing

    lax.fori_loop(0, steps, feed_rows, 0)
    two.second(cuts(steps - 1))
    gain_ref[...] = jnp.zeros_like(gain_ref)

    def shrink_rows(at, nothing):
        lanes = pl.ds(pl.multiple_of(at * 256, 256), 256)
        shrink_parts[pl.ds(at * (256 // own_rows), 256 // own_rows)] = (
            tn(cot_ref[:, lanes], hidden[...]).astype(LOW).reshape(256 // own_rows, own_rows, units)
        )
        return nothing

    lax.fori_loop(0, model // 256, shrink_rows, 0)
    scatter.start(0)
    marks = [1 + (scatter.steps - 1) * at // steps for at in range(steps + 1)]
    for at in range(steps):
        lanes = slice(at * 256, (at + 1) * 256)
        expand_ref[lanes] = tn(second[:, lanes], opened[...]).astype(LOW)
        for step in range(marks[at], (marks[at] + marks[at + 1]) // 2):
            scatter.start(step)
        two.third(cuts(at))
        rows = Pair(length // 2, at, size)
        rows.store(
            mlp_ref,
            nt(rows.load(hidden), columns(back_ref, mixer_rows, mixer_rows + units)).astype(LOW),
        )
        for step in range((marks[at] + marks[at + 1]) // 2, marks[at + 1]):
            scatter.start(step)
        two.landed(cuts(at))
        middle = rows.load(tokens_ref).astype(jnp.float32) + rows.load(mixed_ref).astype(jnp.float32)
        scale = lax.rsqrt(jnp.mean(middle * middle, -1, keepdims=True) + EPS_NORM)
        normal = middle * scale
        arrived = rows.load(total2).astype(jnp.float32)
        scaled = arrived * scales_ref[0:1]
        inner = jnp.mean(normal * scaled, -1, keepdims=True)
        outgoing = rows.load(cot_ref).astype(jnp.float32) + scale * (scaled - normal * inner)
        rows.store(grad_ref, outgoing.astype(LOW))
        gain_ref[0:1] += jnp.sum(arrived * normal, 0, keepdims=True)

    def output_rows(at, nothing):
        lanes = pl.ds(pl.multiple_of(at * 256, 256), 256)
        output_ref[lanes] = tn(grad_ref[:, lanes], gated_all[column]).astype(LOW)
        return nothing

    lax.fori_loop(0, model // 256, output_rows, 0)
    scatter.finish((shrink_share,))
    for at in range(2 * steps):
        sharing.flush(at)
    two.flush()
    ring.drain()


def feed(
    fo, state, projected, gating, back, outs, own, tokens, cotangent, scales, heads, units, ident
):
    length, model = tokens.shape
    count = back.shape[0]
    mixer_rows = heads * DK
    f32 = jnp.float32
    token_block = pltpu.VMEM((length, model), LOW)
    return pl.pallas_call(
        lambda *refs: feed_body(count, heads, scatter_cuts([units], [4]), *refs),
        out_shape=[
            jax.ShapeDtypeStruct((heads, length, DK), f32),
            jax.ShapeDtypeStruct((length, model), LOW),
            jax.ShapeDtypeStruct((length, model), LOW),
            jax.ShapeDtypeStruct((length, model), LOW),
            jax.ShapeDtypeStruct((model, 2 * units), LOW),
            jax.ShapeDtypeStruct((own.shape[0], units), f32),
            jax.ShapeDtypeStruct((model, mixer_rows), LOW),
            jax.ShapeDtypeStruct((8, model), f32),
        ],
        in_specs=[VMEM, VMEM, VMEM, VMEM, ANY, ANY, VMEM, ANY, ANY, VMEM],
        out_specs=[VMEM] * 8,
        scratch_shapes=[
            pltpu.VMEM((4, length, mixer_rows), LOW),
            pltpu.VMEM((count, *own.shape), LOW),
            token_block,
            token_block,
            *head_scratch(length, model),
            pltpu.VMEM((count, own.shape[0], units), LOW),
            pltpu.VMEM((length, units), LOW),
            pltpu.VMEM((length, 2 * units), LOW),
            token_block,
            pltpu.VMEM((length, units), f32),
            *gather_scratch(4, count),
            pltpu.SemaphoreType.DMA((3, 8)),
            pltpu.SemaphoreType.DMA((3, 8)),
            *scatter_scratch(count, [own.shape[0]], [units], [4]),
            *[
                pltpu.VMEM(array.shape, array.dtype) for array in (back, outs, tokens, cotangent)
            ],
            pltpu.SemaphoreType.DMA((4,)),
        ],
        compiler_params=params(ident),
        name="feed",
    )(fo, state, projected, gating, back, outs, own, tokens, cotangent, scales)


def direct_body(
    heads, grad_ref, output_ref, res_ref, x_ref, gating_ref, score_ref, qk_ref, uw_ref, col_ref, row_ref,
    dout_ref, dz_ref, dgating_ref, adj_ref, ddelta_ref, direct_ref,
    carry,
):
    full = (2 + 2 * NH) * DK
    step = pl.program_id(0)

    @pl.when(step == 0)
    def _():
        ones = (
            lax.broadcasted_iota(jnp.int32, (DK, 2 * DK), 0)
            == lax.broadcasted_iota(jnp.int32, (DK, 2 * DK), 1)
        ).astype(jnp.float32)
        for head in range(heads):
            carry[head] = ones
        dgating_ref[...] = jnp.zeros_like(dgating_ref)

    col = col_ref[...]
    grad = mm(grad_ref[...], output_ref[...])
    douts = []
    for head in range(heads):
        result = res_ref[head]
        scale = lax.rsqrt(jnp.mean(result * result, -1, keepdims=True) + EPS_NORM)
        gate = x_ref[:, (head + 1) * full - DK : (head + 1) * full].astype(jnp.float32)
        opened, slope = silu_parts(gate)
        incoming = grad[:, head * DK : (head + 1) * DK]
        gains = gating_ref[head : head + 1]
        normal = result * scale
        dz_ref[:, head * DK : (head + 1) * DK] = (incoming * normal * gains * slope).astype(LOW)
        dgating_ref[head : head + 1] += jnp.sum(incoming * normal * opened, 0, keepdims=True)
        scaled = incoming * gains * opened
        dout = scale * (scaled - normal * jnp.mean(normal * scaled, -1, keepdims=True))
        dout_ref[head] = dout.astype(LOW)
        douts.append(dout)
    chains = [(head, sub) for sub in reversed(range(SUB)) for head in range(heads)]
    work = {}
    for head, sub in chains:
        rows = slice(sub * STRETCH, (sub + 1) * STRETCH)
        unused, unused, beta, unused, unused, initial, last, keep = chain_scalars(
            col, row_ref[sub], head, rows, heads
        )
        queries = qk_ref[head, sub, :STRETCH].astype(jnp.float32) * initial[:STRETCH]
        both = tn(
            jnp.concatenate([queries.astype(LOW), score_ref[head, sub]], 1), douts[head][rows]
        )
        keys = qk_ref[head, sub, STRETCH:].astype(jnp.float32) * last
        work[head, sub] = (both[:DK], both[DK:], keys, keep)
    for head, sub in chains:
        into, ddelta, keys, keep = work[head, sub]
        adjoint = carry[head]
        adj_ref[head, sub] = adjoint.astype(LOW)
        moved = mm(keys, adjoint)
        ddelta = jnp.concatenate([moved[:, :DK], ddelta + moved[:, DK:]], 1)
        ddelta_ref[head, sub] = ddelta.astype(LOW)
        back = keep * adjoint - tn(uw_ref[head, sub, :, DK:], ddelta)
        carry[head] = jnp.concatenate([back[:, :DK], back[:, DK:] + into], 1)
    direct_ref[...] = carry[...]


def mixer_direct(grad_mixed, output, res, projected, gating, score, qk, uw, col, row, heads):
    length, columns = projected.shape
    rows = SUB * STRETCH
    grid = length // rows
    blocks = length // STRETCH
    steps = NH * STRETCH
    f32 = jnp.float32
    shapes = [
        ((heads, length, DK), LOW, (heads, rows, DK), 1),
        ((length, heads * DK), LOW, (rows, heads * DK), 0),
        ((8, DK), f32, (8, DK), None),
        ((heads, blocks, DK, 2 * DK), LOW, (heads, SUB, DK, 2 * DK), 1),
        ((heads, blocks, steps, 2 * DK), LOW, (heads, SUB, steps, 2 * DK), 1),
        ((heads, DK, 2 * DK), f32, (heads, DK, 2 * DK), None),
    ]
    return pl.pallas_call(
        lambda *refs: direct_body(heads, *refs),
        grid=(grid,),
        out_shape=[jax.ShapeDtypeStruct(s[0], s[1]) for s in shapes],
        in_specs=[
            block_spec((rows, grad_mixed.shape[1]), 0, grid),
            whole_spec((output.shape[0], heads * DK)),
            block_spec((heads, rows, DK), 1, grid),
            block_spec((rows, columns), 0, grid),
            whole_spec(gating.shape),
            block_spec((heads, SUB, STRETCH, steps), 1, grid),
            block_spec((heads, SUB, STRETCH + steps, DK), 1, grid),
            block_spec((heads, SUB, steps, 2 * DK), 1, grid),
            block_spec((rows, 128), 0, grid),
            block_spec((SUB, *row.shape[1:]), 0, grid),
        ],
        out_specs=[
            whole_spec(s[2]) if s[3] is None else block_spec(s[2], s[3], grid) for s in shapes
        ],
        scratch_shapes=[pltpu.VMEM((heads, DK, 2 * DK), f32)],
        compiler_params=pltpu.CompilerParams(vmem_limit_bytes=LIMIT),
        name="mixer_direct",
    )(grad_mixed, output, res, projected, gating, score, qk, uw, col, row)


def row_sum(values):
    return jnp.sum(values, -1, keepdims=True)


def backward_body(
    steps_here, ring_count, cuts, heads, x_ref, before_ref, hist_ref, taps_ref, col_ref, row_ref, mask_ref, pre_ref, t_ref, uw_ref,
    aug_ref, delta_ref, qk_ref, dout_ref, dz_ref, adj_ref, ddelta_ref, state_ref, later_ref,
    coeff_ref, decay_ref, project_hbm, expand_ref, output_ref,
    dx_ref, tail_ref, dhist_ref, dtaps_ref, ddecay_ref, normed_ref, expand_share, output_share,
    line, shift, project_ref, project_load, kept_dx, sent, total, near, half, far, head_send, head_receive, *ring_scratch,
):
    seg_lane = (NH + 1) * heads
    width = (1 + 2 * NH) * DK
    full = (2 + 2 * NH) * DK
    step = pl.program_id(0)
    count = pl.num_programs(0)
    length = x_ref.shape[0]
    chunks = steps_here - 2
    summing = ChunkSum(chunks, sent, total, near, half, far, head_send, head_receive)
    load_project = pltpu.make_async_copy(project_hbm, project_ref, project_load)
    early = range(0, len(cuts) // 2)
    later = range(len(cuts) // 2, len(cuts))
    ring = Scatter(
        ring_count, (expand_ref, output_ref), ring_scratch[:2], ring_scratch[2:4], cuts,
        *ring_scratch[4:],
    )

    @pl.when(step == 0)
    def _():
        load_project.start()
        greet((*head_neighbours(), *ring_neighbours(ring_count)))

    along_grid(step, steps_here, ring.steps, lambda number: ring.start(number, early))
    for chunk in range(0, chunks, 2):

        @pl.when(step == chunk + 3)
        def _():
            summing.second(chunk)
            summing.second(chunk + 1)

        if chunk + 5 < steps_here:

            @pl.when(step == chunk + 5)
            def _():
                summing.third(chunk)
                summing.third(chunk + 1)

    @pl.when(step == 0)
    def _():
        shift[...] = jnp.zeros_like(shift)
        dtaps_ref[...] = jnp.zeros_like(dtaps_ref)
        ddecay_ref[...] = jnp.zeros_like(ddecay_ref)

    @pl.when(step == count - 1)
    def _():
        line[:8] = hist_ref[...]

    col = col_ref[...]
    strict, reach = mask_ref[LEVELS], mask_ref[LEVELS + 1]
    lanes128 = lax.broadcasted_iota(jnp.int32, (STRETCH, 128), 1)
    lane_row = lax.broadcasted_iota(jnp.int32, (1, 128), 1)
    tall = lax.broadcasted_iota(jnp.int32, (128, 128), 0)
    wide = lax.broadcasted_iota(jnp.int32, (128, 128), 1)
    by_row = jnp.zeros((128, 128), jnp.float32)
    dcols = [jnp.zeros((STRETCH, 128), jnp.float32) for _ in range(SUB)]
    slopes, dacts = [], []
    for head in range(heads):
        lanes = slice(head * width, (head + 1) * width)
        activated, slope = silu_parts(pre_ref[:, lanes])
        slopes.append(slope)
        per_sub = []
        for sub in range(SUB):
            rows = slice(sub * STRETCH, (sub + 1) * STRETCH)
            queries, keys, values, scales = head_values(activated, rows)
            cum_col, seg_col, beta, cum_row, seg_row, initial, last, keep = chain_scalars(
                col, row_ref[sub], head, rows, heads
            )
            kept = retained(cum_col, seg_col, cum_row, seg_row, reach)
            gram = nt(qk_ref[head, sub], qk_ref[head, sub, STRETCH:])
            aug, delta_aug = aug_ref[head, sub], delta_ref[head, sub]
            moved = mm(jnp.concatenate([aug[:, :DK], delta_aug[:, :DK]], 0), state_ref[head])
            state = aug[:, DK:].astype(jnp.float32) + moved[:DK]
            delta = delta_aug[:, DK:].astype(jnp.float32) + moved[DK:]
            adj, ddelta_aug = adj_ref[head, sub], ddelta_ref[head, sub]
            moved = mm(jnp.concatenate([adj[:, :DK], ddelta_aug[:, :DK]], 0), later_ref[head])
            dstate = adj[:, DK:].astype(jnp.float32) + moved[:DK]
            ddelta = ddelta_aug[:, DK:].astype(jnp.float32) + moved[DK:]
            dcarried = -nt(ddelta, state)
            dright = tn(t_ref[head, sub], jnp.concatenate([ddelta, dcarried], 1))
            dvalue, dkey = dright[:, :DK], dright[:, DK:]
            dlower = -nt(dright, uw_ref[head, sub])
            dout = dout_ref[head, rows]
            from_out = nt(dout, jnp.concatenate([state, delta], 0))
            dquery = from_out[:, :DK]
            dinitial = row_sum(dquery * queries)
            dgram = from_out[:, DK:] * kept[:STRETCH]
            by_score = dgram * gram[:STRETCH]
            dquery = dquery * initial[:STRETCH] + mm(dgram, keys)
            dlasting = nt(delta, dstate)
            dlast = row_sum(keys * dlasting) * last
            dstrict = dlower * kept * strict
            by_lower = dstrict * gram[STRETCH:]
            dkk = dstrict * beta
            dbeta = row_sum(by_lower)
            key_sum = row_sum(keys * dkey)
            dcum = (
                beta * dbeta
                + beta * initial * key_sum
                - dlast
            )
            dbeta = dbeta + row_sum(values * dvalue) + initial * key_sum
            dkeys = (
                last * dlasting
                + tn(dgram, queries)
                + mm(dkk + dkk.T, keys)
                + (beta * initial) * dkey
            )
            dcum = (
                dcum[:STRETCH]
                + dcum[STRETCH:]
                + row_sum(by_score)
                + dinitial * initial[:STRETCH]
            )
            at_end = jnp.sum(dlast, 0, keepdims=True) + keep * jnp.sum(
                row_sum(state * dstate), 0, keepdims=True
            )
            base = (NH + 1) * head
            part = (
                jnp.where(lane_row == STRETCH - 1, at_end, 0.0)
                - jnp.sum(by_lower * beta, 0, keepdims=True)
                - jnp.sum(by_score, 0, keepdims=True)
            )
            part = part + pltpu.roll(part, STRETCH, 1)
            by_row = jnp.where((tall == base + NH) & (wide // STRETCH == sub), part, by_row)
            dcols[sub] = jnp.where(lanes128 == base + NH, dcum, dcols[sub])
            for j in range(NH):
                dcols[sub] = jnp.where(
                    lanes128 == base + j, dbeta[j * STRETCH : (j + 1) * STRETCH], dcols[sub]
                )
            dkeys = scales * (dkeys - keys * row_sum(keys * dkeys))
            dvalues = beta * dvalue
            per_sub.append(
                jnp.concatenate(
                    [dquery]
                    + [dkeys[j * STRETCH : (j + 1) * STRETCH] for j in range(NH)]
                    + [dvalues[j * STRETCH : (j + 1) * STRETCH] for j in range(NH)],
                    1,
                )
            )
        dacts.append(jnp.concatenate(per_sub, 0))
    along_grid(step, steps_here, ring.steps, lambda number: ring.start(number, later))
    grads = jnp.concatenate(dcols, 0) + by_row.T
    coeff = coeff_ref[...].astype(jnp.float32)
    soft, shifted = decay_terms(coeff, decay_ref[...])
    rate = -decay_ref[0:1]
    rate_lane = (wide < seg_lane) & (wide % (NH + 1) == NH)
    dlog = jnp.where(rate_lane, exact(block_triangle(128), grads, ((0,), (0,))), 0.0)
    dlogit = dlog * rate / (1.0 + jnp.exp(-shifted))
    ddecay_ref[0:1] += jnp.sum(dlog * rate * soft, 0, keepdims=True)
    ddecay_ref[1:2] += jnp.sum(dlogit, 0, keepdims=True)
    dcoeff = jnp.where(rate_lane, dlogit, jnp.where(wide < seg_lane, grads * col * (1.0 - col), 0.0))
    dx_ref[:, heads * full :] = dcoeff.astype(LOW)

    for head in range(heads):
        lanes = slice(head * width, (head + 1) * width)
        line[8:, lanes] = x_ref[:, head * full : head * full + width].astype(jnp.float32)

        @pl.when(step < count - 1)
        def _():
            line[:8, lanes] = before_ref[:, head * full : head * full + width].astype(jnp.float32)[8:]

        dsum = dacts[head] * slopes[head]
        moved_back = dsum * taps_ref[CONV - 1 : CONV, lanes]
        dtaps_ref[CONV - 1 : CONV, lanes] += jnp.sum(dsum * line[8:, lanes], 0, keepdims=True)
        early = jnp.zeros((8, width), jnp.float32)
        for back in range(1, CONV):
            tap = taps_ref[CONV - 1 - back : CONV - back, lanes]
            kept = jnp.where(col[:, seg_lane + back : seg_lane + back + 1] > 0.0, dsum, 0.0)
            dtaps_ref[CONV - 1 - back : CONV - back, lanes] += jnp.sum(
                kept * line[8 - back : 8 - back + length, lanes], 0, keepdims=True
            )
            shift[back - 1, 8 + length :, lanes] = shift[back - 1, 8:16, lanes]
            shift[back - 1, 8 : 8 + length, lanes] = kept
            moved_back = moved_back + tap * shift[back - 1, 8 + back : 8 + back + length, lanes]
            early = early + tap * shift[back - 1, back : back + 8, lanes]
        dx_ref[:, head * full : head * full + width] = moved_back.astype(LOW)
        dx_ref[:, head * full + width : (head + 1) * full] = dz_ref[:, head * DK : (head + 1) * DK]
        dhist_ref[:, lanes] = early

        @pl.when(step == 0)
        def _():
            tail_ref[:, lanes] = moved_back[length - 8 :]

    for chunk in range(0, chunks, 2):

        @pl.when(step == chunk + 1)
        def _():
            kept_dx[:length] = dx_ref[...]

        @pl.when(step == chunk + 2)
        def _():
            kept_dx[length:] = dx_ref[...]
            if chunk == 0:
                load_project.wait()
            both = nt(kept_dx[...], project_ref[...]).astype(LOW)
            sent[chunk] = both[:length]
            sent[chunk + 1] = both[length:]
            summing.first(chunk)
            summing.first(chunk + 1)

    @pl.when(step == count - 1)
    def _():
        summing.third(chunks - 2)
        summing.third(chunks - 1)
        ring.finish((expand_share, output_share))
        summing.finish()
        normed_ref[...] = total[...]


def mixer_backward(
    projected, history, taps, col, row, masks, pre, solved, uw, aug, delta, qk, dout, dz, adj, ddelta,
    state, later, coeff, decay, project, scattered, heads, ring_count, ident,
):
    length, columns = projected.shape
    rows = SUB * STRETCH
    grid = length // rows
    blocks = length // STRETCH
    steps = NH * STRETCH
    conv = history.shape[1]
    f32 = jnp.float32
    shapes = [
        ((length, columns + 128), LOW, (rows, columns + 128), 0),
        ((8, conv), f32, (8, conv), None),
        ((8, conv), f32, (8, conv), None),
        ((8, conv), f32, (8, conv), None),
        ((8, 128), f32, (8, 128), None),
        ((grid - 2, rows, project.shape[0]), LOW, (grid - 2, rows, project.shape[0]), None),
        *[(part.shape[1:], f32, part.shape[1:], None) for part in scattered],
    ]
    widths = [part.shape[-1] for part in scattered]
    own_rows = scattered[0].shape[1]
    pieces_of = (4, 2)
    wide = (heads, SUB, steps, 2 * DK)
    return pl.pallas_call(
        lambda *refs: backward_body(
            grid, ring_count, scatter_cuts(widths, pieces_of), heads, *refs
        ),
        grid=(grid,),
        out_shape=[jax.ShapeDtypeStruct(s[0], s[1]) for s in shapes],
        in_specs=[
            block_spec((rows, columns), 0, grid),
            pl.BlockSpec(
                (16, columns), lambda step: (jnp.maximum((grid - 1 - step) * (rows // 16) - 1, 0), 0)
            ),
            whole_spec(history.shape),
            whole_spec(taps.shape),
            block_spec((rows, 128), 0, grid),
            block_spec((SUB, *row.shape[1:]), 0, grid),
            whole_spec(masks.shape),
            block_spec((rows, conv), 0, grid),
            block_spec((heads, SUB, steps, steps), 1, grid),
            block_spec(wide, 1, grid),
            block_spec((heads, SUB, DK, 2 * DK), 1, grid),
            block_spec(wide, 1, grid),
            block_spec((heads, SUB, STRETCH + steps, DK), 1, grid),
            block_spec((heads, rows, DK), 1, grid),
            block_spec((rows, heads * DK), 0, grid),
            block_spec((heads, SUB, DK, 2 * DK), 1, grid),
            block_spec(wide, 1, grid),
            whole_spec(state.shape),
            whole_spec(later.shape),
            block_spec((rows, 128), 0, grid),
            whole_spec(decay.shape),
            ANY,
            VMEM,
            VMEM,
        ],
        out_specs=[
            whole_spec(s[2]) if s[3] is None else block_spec(s[2], s[3], grid) for s in shapes
        ],
        scratch_shapes=[
            pltpu.VMEM((8 + rows, conv), f32),
            pltpu.VMEM((CONV - 1, 16 + rows, conv), f32),
            pltpu.VMEM(project.shape, LOW),
            pltpu.SemaphoreType.DMA,
            pltpu.VMEM((2 * rows, columns + 128), LOW),
            *[pltpu.VMEM((grid - 2, rows, project.shape[0]), LOW)] * 5,
            *[pltpu.SemaphoreType.DMA((3, grid - 2))] * 2,
            *scatter_scratch(ring_count, [own_rows] * 2, widths, pieces_of),
        ],
        compiler_params=params(ident),
        name="mixer_backward",
    )(
        projected, projected, history, taps, col, row, masks, pre, solved, uw, aug, delta, qk, dout, dz,
        adj, ddelta, state, later, coeff, decay, project, *scattered,
    )


def adamw(weight, first, second, gradient, factor, step_rate, decay_rate):
    gradient = gradient * factor
    moment = BETA_ONE * first + (1.0 - BETA_ONE) * gradient
    square = BETA_TWO * second + (1.0 - BETA_TWO) * gradient * gradient
    scaled = moment / (1.0 - BETA_ONE**STEP)
    spread = jnp.sqrt(square / (1.0 - BETA_TWO**STEP))
    master = weight - step_rate * (scaled / (spread + ADAM_EPS) + decay_rate * weight)
    return (master, moment, square)


def on_device(
    tokens,
    cotangent,
    row_starts,
    project_weight,
    project_first,
    project_second,
    coeffs_weight,
    coeffs_first,
    coeffs_second,
    kernel_weight,
    kernel_first,
    kernel_second,
    output_weight,
    output_first,
    output_second,
    expand_weight,
    expand_first,
    expand_second,
    reduce_weight,
    reduce_first,
    reduce_second,
    scales_weight,
    scales_first,
    scales_second,
    gating_weight,
    gating_first,
    gating_second,
    decays_weight,
    decays_first,
    decays_second,
):
    heads_here = H // lax.axis_size("head")
    head_index = lax.axis_index("head")
    width = (1 + 2 * NH) * DK
    full = (2 + 2 * NH) * DK
    spans = lax.axis_size("seq")
    own_rows, columns_here = project_weight.shape
    units = expand_weight.shape[2]
    padded_units = -(-units // 256) * 256
    mixer_rows = heads_here * DK
    coeff_count = coeffs_weight.shape[1]
    kernel_columns = kernel_weight.shape[1]
    gating_columns = gating_weight.shape[1]
    tiny_columns = -(-max(kernel_columns, own_rows) // 128) * 128

    def pack_tiny(kernel_part, scales_part, gating_part, kind):
        lead = [(0, 0)] * (kernel_part.ndim - 2)
        parts = [
            jnp.pad(part, lead + [(0, 0), (0, tiny_columns - part.shape[-1])])
            for part in (kernel_part, scales_part, gating_part)
        ]
        stacked = jnp.concatenate(parts, -2)
        return jnp.pad(stacked, lead + [(0, 16 - stacked.shape[-2]), (0, 0)]).astype(kind)

    def unpack_tiny(block):
        return (
            block[..., :heads_here, :kernel_columns],
            block[..., heads_here : heads_here + 2, :own_rows],
            block[..., heads_here + 2 : 2 * heads_here + 2, :gating_columns],
        )

    length = tokens.shape[0]
    model = spans * own_rows
    (
        mixer_whole, tinies, normed, projected, coeff, col, row, history, own_back, own_rest,
        decay_table,
    ) = enter(
        project_weight, coeffs_weight.T, kernel_weight, scales_weight, gating_weight, output_weight,
        reduce_weight, expand_weight.transpose(1, 2, 0), decays_weight, tokens,
        row_starts.reshape(-1, 128), spans, heads_here, padded_units, tiny_columns, 1,
    )
    kernel_low, scales_low, gating_low = [
        jnp.moveaxis(part, 0, -2).reshape(part.shape[1], -1).astype(jnp.float32)
        for part in unpack_tiny(tinies)
    ]
    taps = jnp.pad(
        kernel_low.reshape(heads_here, width, CONV).transpose(2, 0, 1).reshape(CONV, -1),
        ((0, 8 - CONV), (0, 0)),
    )
    scales_table = jnp.repeat(scales_low, 8, 0)
    gating = jnp.pad(gating_low, ((0, 8 - heads_here), (0, 0)))
    masks = jnp.asarray(block_masks())
    pre, solved, uw, aug, delta, score, qk, fo, span, back_whole = mixer_forward(
        projected, history, taps, col, row, masks, own_back, heads_here, spans, 10
    )
    span_all, state_in, outs = states_before(span, back_whole, spans, 2)
    (
        results, mixed, mlp_part, grad_mixed, grad_expand, shrink_share, grad_output, gain_two,
    ) = feed(
        fo, state_in, projected, gating, back_whole, outs, own_rest, tokens, cotangent,
        scales_table[8:], heads_here, padded_units, 3,
    )
    output = back_whole.reshape(model, -1)
    dout, dz, dgating, adj, ddelta, direct = mixer_direct(
        grad_mixed, output, results, projected, gating, score, qk, uw, col, row, heads_here
    )
    state_grad = states_after(direct[:, :, DK:].astype(jnp.bfloat16), span_all, spans, 4)
    dx, dx_tail, dhistory, dtaps, ddecay, summed, expand_share, output_share = mixer_backward(
        projected, history, taps, col, row, masks, pre, solved, uw, aug, delta, qk, dout, dz, adj,
        ddelta, state_in, state_grad, coeff, decay_table, mixer_whole.reshape(model, -1),
        [
            part.reshape(spans, own_rows, -1) for part in (grad_expand, grad_output)
        ],
        heads_here, spans, 11,
    )
    grad_kernel = dtaps[:CONV].reshape(CONV, heads_here, width).transpose(1, 2, 0)
    def by_owner(array):
        return jnp.moveaxis(array.reshape(array.shape[0], spans, -1), 1, 0)

    small = pack_tiny(
        by_owner(grad_kernel.reshape(heads_here, -1)),
        by_owner(jnp.concatenate([jnp.zeros_like(gain_two[:1]), gain_two[:1]])),
        by_owner(dgating[:heads_here]),
        jnp.float32,
    )
    input_grad, mixer_share, tiny_share, totals, mlp_out = leave(
        dx, dx_tail, dhistory, col, normed, mixer_whole, tokens, grad_mixed, scales_table[:8],
        small, ddecay, expand_share, shrink_share, output_share,
        summed, mlp_part, heads_here, 8,
    )
    news = update(
        (
            mixer_share, expand_share, shrink_share, output_share, tiny_share, totals, tokens,
            mixed, mlp_out,
        ),
        (
            project_weight,
            project_first,
            project_second,
            coeffs_weight.T,
            coeffs_first.T,
            coeffs_second.T,
            kernel_weight,
            kernel_first,
            kernel_second,
            output_weight,
            output_first,
            output_second,
            expand_weight.transpose(1, 2, 0),
            expand_first.transpose(1, 2, 0),
            expand_second.transpose(1, 2, 0),
            reduce_weight,
            reduce_first,
            reduce_second,
            scales_weight,
            scales_first,
            scales_second,
            gating_weight,
            gating_first,
            gating_second,
            decays_weight,
            decays_first,
            decays_second,
        ),
        (heads_here, units, coeff_count, kernel_columns, own_rows, gating_columns),
    )
    coeffs_new = [part.T for part in news[4:8]]
    expand_new = [part.transpose(2, 0, 1) for part in news[16:20]]
    return (
        news[34],
        input_grad,
        *news[:4],
        *coeffs_new,
        *news[8:16],
        *expand_new,
        *news[20:33],
        news[33][0, 0],
    )


def solution(mesh):
    placed = (
        P("seq", None),
        P("seq", None),
        P("seq"),
        P("seq", "head"),
        P("seq", "head"),
        P("seq", "head"),
        P("seq", "head"),
        P("seq", "head"),
        P("seq", "head"),
        P("head", "seq"),
        P("head", "seq"),
        P("head", "seq"),
        P("head", "seq"),
        P("head", "seq"),
        P("head", "seq"),
        P("seq", None, "head"),
        P("seq", None, "head"),
        P("seq", None, "head"),
        P("head", "seq"),
        P("head", "seq"),
        P("head", "seq"),
        P(None, "seq"),
        P(None, "seq"),
        P(None, "seq"),
        P("head", "seq"),
        P("head", "seq"),
        P("head", "seq"),
        P(),
        P(),
        P(),
    )
    return jax.shard_map(
        on_device,
        mesh=mesh,
        in_specs=placed,
        out_specs=(
            P("seq", None),
            P("seq", None),
            P("seq", "head"),
            P("seq", "head"),
            P("seq", "head"),
            P("seq", "head"),
            P("seq", "head"),
            P("seq", "head"),
            P("seq", "head"),
            P("seq", "head"),
            P("head", "seq"),
            P("head", "seq"),
            P("head", "seq"),
            P("head", "seq"),
            P("head", "seq"),
            P("head", "seq"),
            P("head", "seq"),
            P("head", "seq"),
            P("seq", None, "head"),
            P("seq", None, "head"),
            P("seq", None, "head"),
            P("seq", None, "head"),
            P("head", "seq"),
            P("head", "seq"),
            P("head", "seq"),
            P("head", "seq"),
            P(None, "seq"),
            P(None, "seq"),
            P(None, "seq"),
            P("head", "seq"),
            P("head", "seq"),
            P("head", "seq"),
            P(),
            P(),
            P(),
            P(),
        ),
        check_vma=False,
    )
```
